512 devices in a mesh: chol: 16 (over x, z_hi), pair: 32 (over z_lo, y, core).
Axes of the slice: x: 4, y: 4, z: 16 (z_hi: 4, z_lo: 4; z = z_hi * 4 + z_lo), core: 2. Of those that a mesh axis runs over, the one named last changes fastest.
Arguments:
- chol_vectors: bfloat16 [16, 4096, 1024], P(None, ('chol', 'pair')), may hold values from -0.75 to 0.75
- amplitudes: bfloat16 [1024, 64, 1024], P('chol', 'pair'), may hold values from -6 to 6
- fock: bfloat16 [1024, 1024], replicated
- orbital_energy: float32 [16], replicated, may hold values from -1.5 to -0.3
- pair_orbitals: int32 [32, 2], replicated, may hold values from 0 to 15, as said below
- pair_case: int32 [32], replicated, may hold values from 0 to 1
- owner_offsets: int32 [33], replicated, may hold values from 0 to 32, as said below
Outputs:
- residual: float32 [1024, 64, 1024], P('chol', 'pair')
The draws below stay inside these ranges and needn't reach their ends.
Inputs may be any that keep to these rules, and one draw needn't show every extreme that they name: `pair_orbitals`: each row holds two different orbitals, the smaller first. `owner_offsets`: starts at 0, never falls, ends at 32; each owner holds 0 to 2 pairs and some owner holds exactly 2 in every draw.
All inputs are finite; a program needn't handle non-finite values.
Results may differ from the reference program's by a relative error of at most 0.005.
Values may be sent and summed in bfloat16 or wider, within the bound.
No kernel may reach another device: no remote copies, remote signals or barrier semaphores. Data moves between devices by JAX's collectives and lax.ppermute only.
A program may use at most 64 MiB of HBM per device.

```python
import jax
import jax.numpy as jnp
from jax import lax

NV = 1024
NACT = 16
PV_GRP = 256
CAP = 2
NPAIR = 32
NCHOL = 4096
N_CHOL = 16
N_PAIR = 32


def draw_fock(key, part):
    key = jax.random.fold_in(key, 11)
    key_diag, key_rough = jax.random.split(key)
    diagonal = jax.random.uniform(key_diag, (NV,), minval=1.0, maxval=4.0)
    rough = jax.random.normal(key_rough, (NV, NV))
    symmetric = (rough + rough.T) * (0.7 / NV ** 0.5)
    return (symmetric + jnp.diag(diagonal)).astype(jnp.bfloat16)


def draw_pair_orbitals(key, part):
    key = jax.random.fold_in(key, 12)
    key_first, key_step = jax.random.split(key)
    first_orb = jax.random.randint(key_first, (NPAIR,), 0, NACT)
    stride = jax.random.randint(key_step, (NPAIR,), 1, NACT)
    second_orb = (first_orb + stride) % NACT
    return jnp.stack([jnp.minimum(first_orb, second_orb), jnp.maximum(first_orb, second_orb)], axis=1).astype(jnp.int32)


def draw_owner_offsets(key, part):
    key = jax.random.fold_in(key, 13)
    key_perm, key_swing = jax.random.split(key)
    shuffled = jax.random.permutation(key_perm, NPAIR)
    swing = jax.random.randint(key_swing, (NPAIR // 2,), -1, 2)
    swing = swing.at[0].set(1)
    counts = jnp.zeros((NPAIR,), jnp.int32)
    counts = counts.at[shuffled[0::2]].set(1 + swing).at[shuffled[1::2]].set(1 - swing)
    return jnp.concatenate([jnp.zeros((1,), jnp.int32), jnp.cumsum(counts)]).astype(jnp.int32)


def touch_ends(entries, rng, least, top_value):
    longest = entries.shape.index(max(entries.shape))
    spots = []
    for shift in (0, 1):
        where = [jax.random.randint(jax.random.fold_in(rng, axis), (), 0, length) for axis, length in enumerate(entries.shape)]
        where[longest] = (where[longest] + shift) % entries.shape[longest]
        spots.append(tuple(where))
    return entries.at[spots[0]].set(least).at[spots[1]].set(top_value)


def steps_of(rng, shape, shards, least, high):
    factor_of, own = 1.0, jax.random.fold_in(rng, 6)
    for axis_at, parts in shards:
        heights = jnp.exp(jax.random.uniform(jax.random.fold_in(own, axis_at), (parts,), jnp.float32, least / len(shards), high / len(shards)))
        factor_of = factor_of * jnp.repeat(heights, shape[axis_at] // parts).reshape([-1 if axis == axis_at else 1 for axis in range(len(shape))])
    return factor_of


def scatter_about(own_key, shape, scale, limit, cuts=(), kind=jnp.bfloat16):
    drawn = scale * jax.random.normal(own_key, shape, jnp.float32)
    if cuts:
        drawn = drawn * steps_of(own_key, shape, cuts, -0.22, 0.18)
    return jnp.clip(drawn, -limit, limit).astype(kind)


def setup_inputs(seed: int = 0) -> dict:
    key_list = jax.random.split(jax.random.key(seed), 8)
    return {
        "chol_vectors": scatter_about(key_list[0], (NACT, NCHOL, NV), (NCHOL ** -0.25), 0.75, ((1, 512),)),
        "amplitudes": scatter_about(key_list[1], (NV, NPAIR * CAP, NV), 1.0, 6.0, ((0, 16), (1, 32))),
        "fock": draw_fock(jax.random.fold_in(key_list[7], 71), 0),
        "orbital_energy": jnp.clip(jax.random.uniform(key_list[3], (NACT,), jnp.float32, -1.5, -0.3), -1.5, -0.3),
        "pair_orbitals": draw_pair_orbitals(jax.random.fold_in(key_list[7], 71), 0),
        "pair_case": touch_ends(jax.random.randint(key_list[5], (NPAIR,), 0, 2), jax.random.fold_in(key_list[5], 1), 0, 1).astype(jnp.int32),
        "owner_offsets": draw_owner_offsets(jax.random.fold_in(key_list[7], 71), 0),
    }


def reference(chol_vectors, amplitudes, fock, orbital_energy, pair_orbitals, pair_case, owner_offsets):
    pair_ids = jnp.arange(NPAIR, dtype=jnp.int32)
    owners = jnp.sum((owner_offsets[1:][None, :] <= pair_ids[:, None]).astype(jnp.int32), axis=1).astype(jnp.int32)
    slot_ids = (owners * CAP + (pair_ids - owner_offsets[owners])).astype(jnp.int32)
    grouped = chol_vectors.reshape(NACT, N_CHOL, PV_GRP, NV)
    band = NV // N_CHOL
    fock_bands = jnp.transpose(fock.reshape(NV, N_CHOL, band), (1, 0, 2))

    def one_pair(index):
        first_orb = pair_orbitals[index, 0]
        second_orb = pair_orbitals[index, 1]
        coupling = jnp.where(pair_case[index] == 0, 1.0, -1.0).astype(jnp.float32)
        amp = amplitudes[:, slot_ids[index], :]
        amp_bands = amp.reshape(N_CHOL, band, NV)

        def add_group(running, group):
            left_vec, right_vec, fock_band, amp_band = group
            direct = jnp.dot(left_vec.T, right_vec, preferred_element_type=jnp.float32)
            left_part = jnp.dot(fock_band, amp_band, preferred_element_type=jnp.float32)
            partial_sum = 0.5 * (direct + coupling * direct.T) + left_part
            rounded = lax.optimization_barrier(partial_sum.astype(jnp.bfloat16)).astype(jnp.float32)
            return running + rounded, None

        coupled, _ = lax.scan(add_group, jnp.zeros((NV, NV), jnp.float32),
                              (grouped[first_orb], grouped[second_orb], fock_bands, amp_bands))
        right_term = jnp.dot(amp, fock, preferred_element_type=jnp.float32)
        shift = orbital_energy[first_orb] + orbital_energy[second_orb]
        return coupled + right_term - shift * amp.astype(jnp.float32)

    results = lax.map(one_pair, pair_ids)
    full = jnp.zeros((N_PAIR * CAP, NV, NV), jnp.float32).at[slot_ids].set(results)
    return jnp.transpose(full, (1, 0, 2))
```

```python
import jax
import jax.numpy as jnp
from jax import lax
from jax.experimental import pallas as pl
from jax.experimental.pallas import tpu as pltpu
from jax.sharding import Mesh, PartitionSpec as P

CHOL = ("x", "zh")
PAIR = ("zl", "y", "core")
VMEM = pl.BlockSpec(memory_space=pltpu.VMEM)
SMEM = pl.BlockSpec(memory_space=pltpu.SMEM)
LIMIT = pltpu.CompilerParams(vmem_limit_bytes=32 * 1024 * 1024)


def pair_at(zl, y, core):
    return y * 8 + zl * 2 + core


def select_kernel(orbitals, vectors, out):
    for dest in range(32):
        pair = pair_at(dest // 8, dest // 2 % 4, dest % 2)
        out[dest, 0] = vectors[orbitals[0, pair]]
        out[dest, 1] = vectors[orbitals[1, pair]]


def couple_kernel(case, vectors, out):
    pair = pair_at(lax.axis_index("zl"), lax.axis_index("y"), lax.axis_index("core"))
    swap = jnp.where(case[pair] == 0, 0.5, -0.5).astype(jnp.float32)
    left = vectors[:, 0].astype(jnp.float32)
    right = vectors[:, 1].astype(jnp.float32)
    rows = jnp.stack([left, right], axis=1).reshape(512, 1024)
    cols = jnp.stack([0.5 * right, swap * left], axis=1).reshape(512, 1024).astype(jnp.bfloat16)
    for i in range(4):
        block = rows[:, i * 256 : (i + 1) * 256].T.astype(jnp.bfloat16)
        for j in range(4):
            product = jnp.dot(block, cols[:, j * 256 : (j + 1) * 256], preferred_element_type=jnp.float32)
            out[i * 4 + j] = product.astype(jnp.bfloat16)


def route_kernel(offsets, parts, out, total):
    total[...] = jnp.sum(parts[...].astype(jnp.float32), axis=0).astype(jnp.bfloat16)
    member = lax.axis_index("zl") * 2 + lax.axis_index("core")
    for chip in range(16):
        end = offsets[chip * 2 + 2]
        which = jnp.maximum(((end + 7 - member) >> 3) - 1, 0)
        out[chip] = total[which]


def body(chol_vectors, amplitudes, fock, orbital_energy, pair_orbitals, pair_case, owner_offsets):
    zl, y, core = (lax.axis_index(name) for name in PAIR)
    owner = zl * 8 + y * 2 + core
    band = lax.axis_index("x") * 4 + lax.axis_index("zh")
    flat = amplitudes.reshape(64, 2048)
    all_amps = lax.all_gather(flat, CHOL, axis=0, tiled=True)

    chosen = pl.pallas_call(
        select_kernel,
        out_shape=jax.ShapeDtypeStruct((32, 2, 8, 1024), jnp.bfloat16),
        in_specs=[SMEM, VMEM],
        out_specs=VMEM,
        compiler_params=LIMIT,
    )(pair_orbitals.T, chol_vectors)
    vectors = lax.all_to_all(chosen, PAIR, 0, 0, tiled=True)
    partial = pl.pallas_call(
        couple_kernel,
        out_shape=jax.ShapeDtypeStruct((16, 256, 256), jnp.bfloat16),
        in_specs=[SMEM, VMEM],
        out_specs=VMEM,
        compiler_params=LIMIT,
    )(pair_case, vectors)
    parts = lax.all_to_all(partial, ("x", "y"), 0, 0, tiled=True)
    parts = jnp.sum(parts.reshape(4, 4, 4, 64, 256).astype(jnp.float32), axis=0).astype(jnp.bfloat16)
    parts = lax.all_to_all(jnp.swapaxes(parts, 0, 1), "zh", 0, 0, tiled=True)
    routed = pl.pallas_call(
        route_kernel,
        out_shape=jax.ShapeDtypeStruct((16, 64, 256), jnp.bfloat16),
        in_specs=[SMEM, VMEM],
        out_specs=VMEM,
        scratch_shapes=[pltpu.VMEM((4, 64, 256), jnp.bfloat16)],
        compiler_params=LIMIT,
    )(owner_offsets, parts)
    arrived = lax.all_to_all(routed, ("zl", "y"), 0, 0, tiled=True).reshape(4, 4, 64, 256)

    def held(first):
        pair = first + ((first ^ core) & 1)
        return lax.dynamic_index_in_dim(arrived, (pair & 7) >> 1, 0, keepdims=False)

    first = owner_offsets[owner]
    count = owner_offsets[owner + 1] - first
    other = lax.ppermute(held(owner_offsets[owner ^ 1]), "core", [(0, 1), (1, 0)])
    mine = held(first)
    own_first = (first & 1) == core
    slots = [jnp.where(own_first, mine, other), jnp.where(own_first, other, mine)]

    rows = lax.dynamic_slice_in_dim(fock, band * 64, 64, 0)
    left = jnp.dot(rows, all_amps, preferred_element_type=jnp.float32)
    pieces = []
    for slot in range(2):
        pair = jnp.minimum(first + slot, 31)
        shift = orbital_energy[pair_orbitals[pair, 0]] + orbital_energy[pair_orbitals[pair, 1]]
        amp = flat[:, slot * 1024 : (slot + 1) * 1024]
        term = jnp.dot(amp, fock, preferred_element_type=jnp.float32)
        coupled = jnp.swapaxes(slots[slot], 0, 1).reshape(64, 1024).astype(jnp.float32)
        result = coupled + left[:, slot * 1024 : (slot + 1) * 1024] + term - shift * amp.astype(jnp.float32)
        pieces.append(jnp.where(slot < count, result, 0.0))
    return jnp.stack(pieces, axis=1)


def solution(mesh):
    fine = Mesh(mesh.devices.reshape(4, 4, 4, 4, 2), ("x", "zh", "zl", "y", "core"))
    in_specs = (P(None, CHOL + PAIR, None), P(CHOL, PAIR, None), P(), P(), P(), P(), P())
    return jax.shard_map(body, mesh=fine, in_specs=in_specs, out_specs=P(CHOL, PAIR, None), check_vma=False)
```

```python
import jax
import jax.numpy as jnp
from jax import lax
from jax.experimental import pallas as pl
from jax.experimental.pallas import tpu as pltpu
from jax.sharding import Mesh, PartitionSpec as P

CHOL = ("x", "zh")
PAIR = ("zl", "y", "core")
VMEM = pl.BlockSpec(memory_space=pltpu.VMEM)
ANY = pl.BlockSpec(memory_space=pl.ANY)
SMEM = pl.BlockSpec(memory_space=pltpu.SMEM)
LIMIT = pltpu.CompilerParams(vmem_limit_bytes=32 * 1024 * 1024)


def pair_at(zl, y, core):
    return y * 8 + zl * 2 + core


def chol_at(dx, dz):
    return (lax.axis_index("x") ^ dx) * 4 + (lax.axis_index("zh") ^ dz)


def select_kernel(orbitals, vectors, out):
    for dest in range(32):
        pair = pair_at(dest // 8, dest // 2 % 4, dest % 2)
        out[dest, 0] = vectors[orbitals[0, pair]]
        out[dest, 1] = vectors[orbitals[1, pair]]


def split_kernel(amps, out):
    for dx in range(4):
        for dz in range(4):
            start = pl.multiple_of(chol_at(dx, dz) * 128, 128)
            out[dx, dz] = amps[:, pl.ds(start, 128)]


def fock_kernel(fock, *refs):
    blocks, out, columns, product = refs[:4], refs[4], refs[5], refs[6]
    for dz in range(4):
        for dx in range(4):
            start = pl.multiple_of(chol_at(dx, dz) * 64, 64)
            columns[pl.ds(start, 64)] = blocks[dz][dx]
    product[...] = jnp.dot(fock[...], columns[...], preferred_element_type=jnp.float32).astype(jnp.bfloat16)
    for dz in range(4):
        for dx in range(4):
            start = pl.multiple_of(chol_at(dx, dz) * 64, 64)
            out[dz, dx] = product[pl.ds(start, 64)]


def local_kernel(offsets, orbitals, energy, amps, fock, *refs):
    blocks, out = refs[:4], refs[4]
    owner = lax.axis_index("zl") * 8 + lax.axis_index("y") * 2 + lax.axis_index("core")
    for dx in range(4):
        for dz in range(4):
            start = pl.multiple_of(chol_at(dx, dz) * 128, 128)
            out[:, pl.ds(start, 128)] = blocks[dx][dz].astype(jnp.float32)
    for slot in range(2):
        pair = jnp.minimum(offsets[owner] + slot, 31)
        shift = energy[orbitals[0, pair]] + energy[orbitals[1, pair]]
        here = slice(slot * 1024, (slot + 1) * 1024)
        amp = amps[:, here]
        term = jnp.dot(amp, fock[...], preferred_element_type=jnp.float32)
        out[:, here] += term - shift * amp.astype(jnp.float32)


def couple_kernel(case, vectors, *refs):
    out = refs[-1]
    pair = pair_at(lax.axis_index("zl"), lax.axis_index("y"), lax.axis_index("core"))
    swap = jnp.where(case[pair] == 0, 0.5, -0.5).astype(jnp.float32)
    left = vectors[:, 0].astype(jnp.float32)
    right = vectors[:, 1].astype(jnp.float32)
    rows = jnp.stack([left, right], axis=1).reshape(512, 1024)
    cols = jnp.stack([0.5 * right, swap * left], axis=1).reshape(512, 1024).astype(jnp.bfloat16)
    for i in range(4):
        block = rows[:, i * 256 : (i + 1) * 256].T.astype(jnp.bfloat16)
        for j in range(4):
            product = jnp.dot(block, cols[:, j * 256 : (j + 1) * 256], preferred_element_type=jnp.float32)
            out[i * 4 + j] = product.astype(jnp.bfloat16)


def add_kernel(parts, *refs):
    out = refs[-1]
    for y in range(4):
        total = jnp.zeros((256, 256), jnp.float32)
        for x in range(4):
            total += parts[x * 4 + y].astype(jnp.float32)
        for zh in range(4):
            out[zh, y] = total[zh * 64 : (zh + 1) * 64].astype(jnp.bfloat16)


def route_kernel(offsets, parts, *refs):
    out, total = refs[-2:]
    total[...] = jnp.sum(parts[...].astype(jnp.float32), axis=0).astype(jnp.bfloat16)
    member = lax.axis_index("zl") * 2 + lax.axis_index("core")
    for chip in range(16):
        end = offsets[chip * 2 + 2]
        which = jnp.maximum(((end + 7 - member) >> 3) - 1, 0)
        out[chip] = total[which]


def call(kernel, out, in_specs, *args, scratch=()):
    return pl.pallas_call(
        kernel, out_shape=out, in_specs=in_specs, out_specs=VMEM, scratch_shapes=list(scratch), compiler_params=LIMIT
    )(*args)


def half(*shape):
    return jax.ShapeDtypeStruct(shape, jnp.bfloat16)


def exchange(blocks, axis):
    moved = [lax.ppermute(blocks[k], axis, [(i, i ^ k) for i in range(4)]) for k in range(1, 4)]
    return [blocks[0], *moved]


def regroup(blocks):
    return [jnp.stack([block[k] for block in blocks]) for k in range(4)]


def body(chol_vectors, amplitudes, fock, orbital_energy, pair_orbitals, pair_case, owner_offsets):
    zl, y, core = (lax.axis_index(name) for name in PAIR)
    owner = zl * 8 + y * 2 + core
    flat = amplitudes.reshape(64, 2048)
    orbitals = pair_orbitals.T

    chosen = call(select_kernel, half(32, 2, 8, 1024), [SMEM, VMEM], orbitals, chol_vectors)
    vectors = lax.all_to_all(chosen, PAIR, 0, 0, tiled=True)
    columns = exchange(call(split_kernel, half(4, 4, 64, 128), [VMEM], flat), "x")

    partial = call(couple_kernel, half(16, 256, 256), [SMEM, VMEM] + [ANY] * 3, pair_case, vectors, *columns[1:])
    parts = lax.all_to_all(partial, ("x", "y"), 0, 0, tiled=True)
    columns = exchange(regroup(columns), "zh")
    left = call(
        fock_kernel, half(4, 4, 64, 128), [VMEM] * 5, fock, *columns,
        scratch=[pltpu.VMEM((1024, 128), jnp.bfloat16), pltpu.VMEM((1024, 128), jnp.bfloat16)],
    )

    parts = call(add_kernel, half(4, 4, 64, 256), [VMEM, ANY], parts, left)
    parts = lax.all_to_all(parts, "zh", 0, 0, tiled=True)
    left = exchange(left, "zh")

    routed = call(
        route_kernel, half(16, 64, 256), [SMEM, VMEM] + [ANY] * 3, owner_offsets, parts, *left[1:],
        scratch=[pltpu.VMEM((4, 64, 256), jnp.bfloat16)],
    )
    arrived = lax.all_to_all(routed, ("zl", "y"), 0, 0, tiled=True).reshape(4, 4, 64, 256)
    left = exchange(regroup(left), "x")
    local = call(
        local_kernel, jax.ShapeDtypeStruct((64, 2048), jnp.float32), [SMEM] * 3 + [VMEM] * 6,
        owner_offsets, orbitals, orbital_energy, flat, fock, *left,
    )

    def held(first):
        pair = first + ((first ^ core) & 1)
        return lax.dynamic_index_in_dim(arrived, (pair & 7) >> 1, 0, keepdims=False)

    first = owner_offsets[owner]
    count = owner_offsets[owner + 1] - first
    other = lax.ppermute(held(owner_offsets[owner ^ 1]), "core", [(0, 1), (1, 0)])
    mine = held(first)
    own_first = (first & 1) == core
    slots = [jnp.where(own_first, mine, other), jnp.where(own_first, other, mine)]
    pieces = []
    for slot in range(2):
        coupled = jnp.swapaxes(slots[slot], 0, 1).reshape(64, 1024).astype(jnp.float32)
        result = coupled + local[:, slot * 1024 : (slot + 1) * 1024]
        pieces.append(jnp.where(slot < count, result, 0.0))
    return jnp.stack(pieces, axis=1)


def solution(mesh):
    fine = Mesh(mesh.devices.reshape(4, 4, 4, 4, 2), ("x", "zh", "zl", "y", "core"))
    in_specs = (P(None, CHOL + PAIR, None), P(CHOL, PAIR, None), P(), P(), P(), P(), P())
    return jax.shard_map(body, mesh=fine, in_specs=in_specs, out_specs=P(CHOL, PAIR, None), check_vma=False)
```

```python
import jax
import jax.numpy as jnp
from jax import lax
from jax.experimental import pallas as pl
from jax.experimental.pallas import tpu as pltpu
from jax.sharding import Mesh, PartitionSpec as P

CHOL = ("x", "zh")
PAIR = ("zl", "y", "core")
VMEM = pl.BlockSpec(memory_space=pltpu.VMEM)
ANY = pl.BlockSpec(memory_space=pl.ANY)
TURNS = ("zh", "zh")
SMEM = pl.BlockSpec(memory_space=pltpu.SMEM)
LIMIT = pltpu.CompilerParams(vmem_limit_bytes=32 * 1024 * 1024)


def pair_at(zl, y, core):
    return y * 8 + zl * 2 + core


def owner_index():
    return lax.axis_index("zl") * 8 + lax.axis_index("y") * 2 + lax.axis_index("core")


def first_at(offsets, chip, core):
    first = offsets[chip * 2]
    return first + ((first ^ core) & 1)


def prepare_kernel(offsets, orbitals, vectors, other_vectors, amps, other_amps, *refs):
    out, held = refs[-2:]
    core = lax.axis_index("core")
    for dest in range(16):
        pair = pair_at(dest // 4, dest % 4, core)
        for side in range(2):
            for which, source in enumerate((vectors, other_vectors)):
                chosen = source[orbitals[side, pair]]
                for part in range(4):
                    out[dest, side * 8 + which * 4 + part] = chosen[:, part * 256 : (part + 1) * 256]
    for slot in range(2):
        here = slice(slot * 1024, (slot + 1) * 1024)
        held[core * 2 + slot] = amps[:, here]
        held[(1 - core) * 2 + slot] = other_amps[:, here]
    chip = lax.axis_index("zl") * 4 + lax.axis_index("y")
    middle = offsets[chip * 2 + 1]
    for j in range(2):
        pair = first_at(offsets, chip, core) + 2 * j
        late = pair >= middle
        slot = jnp.clip(jnp.where(late, pair - middle, pair - offsets[chip * 2]), 0, 1)
        wide = held[late.astype(jnp.int32) * 2 + slot].astype(jnp.float32)
        for dest in range(16):
            for part in range(2):
                start = dest % 2 * 512 + part * 256
                tile = wide[dest // 2 * 8 : (dest // 2 + 1) * 8, start : start + 256]
                out[dest, 16 + j * 2 + part] = tile.astype(jnp.bfloat16)


def collect_kernel(offsets, arrived, out):
    core = lax.axis_index("core")
    for chip in range(16):
        for j in range(2):
            pair = first_at(offsets, chip, core) + 2 * j

            @pl.when(pair < offsets[chip * 2 + 2])
            def _():
                dest = ((pair & 7) >> 1) * 4 + (pair >> 3)
                for part in range(2):
                    out[dest, part] = arrived[chip, 16 + j * 2 + part]


def local_kernel(offsets, orbitals, energy, amps, fock, out):
    owner = owner_index()
    both = jnp.concatenate([amps[:, :1024], amps[:, 1024:]], axis=0)
    term = jnp.dot(both, fock[...], preferred_element_type=jnp.float32)
    for slot in range(2):
        pair = jnp.minimum(offsets[owner] + slot, 31)
        shift = energy[orbitals[0, pair]] + energy[orbitals[1, pair]]
        amp = both[slot * 64 : (slot + 1) * 64].astype(jnp.float32)
        out[:, slot * 1024 : (slot + 1) * 1024] = term[slot * 64 : (slot + 1) * 64] - shift * amp


def couple_kernel(case, arrived, amp_tiles, fock, out, rows, cols):
    pair = pair_at(lax.axis_index("zl"), lax.axis_index("y"), lax.axis_index("core"))
    x, zh = lax.axis_index("x"), lax.axis_index("zh")
    swap = jnp.where(case[pair] == 0, 0.5, -0.5).astype(jnp.float32)
    cols[512:640] = jnp.zeros((128, 1024), jnp.bfloat16)
    top = pl.multiple_of(512 + (zh & 1) * 64, 64)
    for part in range(4):
        here = slice(part * 256, (part + 1) * 256)
        for which in range(2):
            left = arrived[:, which * 4 + part].astype(jnp.float32).reshape(128, 256)
            right = arrived[:, 8 + which * 4 + part].astype(jnp.float32).reshape(128, 256)
            start = which * 128
            rows[start : start + 128, here] = left
            rows[start + 256 : start + 384, here] = right
            cols[start : start + 128, here] = (0.5 * right).astype(jnp.bfloat16)
            cols[start + 256 : start + 384, here] = (swap * left).astype(jnp.bfloat16)
        tiles = [amp_tiles[group * 2 + part // 2, part % 2].astype(jnp.float32) for group in range(8)]
        cols[pl.ds(top, 64), here] = jnp.concatenate(tiles, axis=0).astype(jnp.bfloat16)
    lanes = pl.multiple_of((x * 2 + (zh >> 1)) * 128, 128)
    for row in range(4):
        here = slice(row * 256, (row + 1) * 256)
        block = jnp.concatenate([rows[:, here].T.astype(jnp.bfloat16), fock[here, pl.ds(lanes, 128)]], axis=1)
        product = jnp.dot(block, cols[...], preferred_element_type=jnp.float32)
        out[row] = product.astype(jnp.bfloat16)


def finish_kernel(parts, out):
    for y in range(4):
        here = slice(y * 256, (y + 1) * 256)
        total = parts[0, :, here].astype(jnp.float32)
        for x in range(1, 4):
            total += parts[x, :, here].astype(jnp.float32)
        for zh in range(4):
            out[zh * 4 + y] = total[zh * 64 : (zh + 1) * 64].astype(jnp.bfloat16)


def route_kernel(offsets, parts, out, total):
    for y in range(4):
        sums = parts[y].astype(jnp.float32)
        for zh in range(1, 4):
            sums += parts[zh * 4 + y].astype(jnp.float32)
        total[y] = sums.astype(jnp.bfloat16)
    member = lax.axis_index("zl") * 2 + lax.axis_index("core")
    for chip in range(16):
        end = offsets[chip * 2 + 2]
        which = jnp.maximum(((end + 7 - member) >> 3) - 1, 0)
        out[chip] = total[which]


def pick_kernel(offsets, arrived, mine, theirs):
    core, owner = lax.axis_index("core"), owner_index()
    for who, out in ((owner, mine), (owner ^ 1, theirs)):
        first = offsets[who]
        pair = first + ((first ^ core) & 1)
        for y in range(4):
            out[:, y * 256 : (y + 1) * 256] = arrived[((pair & 7) >> 1) * 4 + y]


def write_kernel(offsets, mine, other, local, out):
    owner = owner_index()
    first = offsets[owner]
    count = offsets[owner + 1] - first
    for slot in range(2):
        own = ((first + slot) & 1) == lax.axis_index("core")
        coupled = jnp.where(own, mine[...].astype(jnp.float32), other[...].astype(jnp.float32))
        result = coupled + local[:, slot * 1024 : (slot + 1) * 1024]
        out[:, slot, :] = jnp.where(slot < count, result, 0.0)


def call(kernel, out, in_specs, *args, scratch=()):
    return pl.pallas_call(
        kernel,
        out_shape=out,
        in_specs=in_specs,
        out_specs=jax.tree.map(lambda _: VMEM, out),
        scratch_shapes=list(scratch),
        compiler_params=LIMIT,
    )(*args)


def half(*shape):
    return jax.ShapeDtypeStruct(shape, jnp.bfloat16)


def single(*shape):
    return jax.ShapeDtypeStruct(shape, jnp.float32)


def body(chol_vectors, amplitudes, fock, orbital_energy, pair_orbitals, pair_case, owner_offsets):
    flat = amplitudes.reshape(64, 2048)
    orbitals = pair_orbitals.T

    other_vectors, other_flat = lax.ppermute((chol_vectors, flat), "core", [(0, 1), (1, 0)])
    token = orbital_energy
    for axis in TURNS:
        token = lax.ppermute(token, (axis, "core"), [(i * 2 + 1, (i + 1) % 4 * 2 + 1) for i in range(4)])
    chosen = call(
        prepare_kernel, half(16, 20, 8, 256), [SMEM] * 2 + [VMEM] * 4 + [ANY],
        owner_offsets, orbitals, chol_vectors, other_vectors, flat, other_flat, token,
        scratch=[pltpu.VMEM((4, 64, 1024), jnp.bfloat16)],
    )
    arrived = lax.all_to_all(chosen, ("zl", "y"), 0, 0, tiled=True)
    tiles = call(collect_kernel, half(16, 2, 8, 256), [SMEM, VMEM], owner_offsets, arrived)
    tiles = lax.all_to_all(tiles, ("zl", "y"), 0, 0, tiled=True)
    partial = call(
        couple_kernel, half(4, 256, 1024), [SMEM, VMEM, VMEM, VMEM], pair_case, arrived, tiles, fock,
        scratch=[pltpu.VMEM((512, 1024), jnp.float32), pltpu.VMEM((640, 1024), jnp.bfloat16)],
    )
    parts = lax.all_to_all(partial, "x", 0, 0, tiled=True)
    parts = call(finish_kernel, half(16, 64, 256), [VMEM], parts)
    parts = lax.all_to_all(parts, ("zh", "y"), 0, 0, tiled=True)
    routed = call(
        route_kernel, half(16, 64, 256), [SMEM, VMEM], owner_offsets, parts,
        scratch=[pltpu.VMEM((4, 64, 256), jnp.bfloat16)],
    )
    arrived = lax.all_to_all(routed, ("zl", "y"), 0, 0, tiled=True)
    mine, theirs = call(pick_kernel, [half(64, 1024), half(64, 1024)], [SMEM, VMEM], owner_offsets, arrived)
    other = lax.ppermute(theirs, "core", [(0, 1), (1, 0)])
    local = call(
        local_kernel, single(64, 2048), [SMEM] * 3 + [VMEM] * 2, owner_offsets, orbitals, orbital_energy, flat, fock
    )
    return call(write_kernel, single(64, 2, 1024), [SMEM] + [VMEM] * 3, owner_offsets, mine, other, local)


def solution(mesh):
    fine = Mesh(mesh.devices.reshape(4, 4, 4, 4, 2), ("x", "zh", "zl", "y", "core"))
    in_specs = (P(None, CHOL + PAIR, None), P(CHOL, PAIR, None), P(), P(), P(), P(), P())
    return jax.shard_map(body, mesh=fine, in_specs=in_specs, out_specs=P(CHOL, PAIR, None), check_vma=False)
```

```python
import jax
import jax.numpy as jnp
from jax import lax
from jax.experimental import pallas as pl
from jax.experimental.pallas import tpu as pltpu
from jax.sharding import Mesh, PartitionSpec as P

CHOL = ("x", "zh")
PAIR = ("zl", "y", "core")
VMEM = pl.BlockSpec(memory_space=pltpu.VMEM)
ANY = pl.BlockSpec(memory_space=pl.ANY)
TURNS = ("zh",)
AFTER = False
SMEM = pl.BlockSpec(memory_space=pltpu.SMEM)
LIMIT = pltpu.CompilerParams(vmem_limit_bytes=32 * 1024 * 1024)


def pair_at(zl, y, core):
    return y * 8 + zl * 2 + core


def owner_index():
    return lax.axis_index("zl") * 8 + lax.axis_index("y") * 2 + lax.axis_index("core")


def first_at(offsets, chip, core):
    first = offsets[chip * 2]
    return first + ((first ^ core) & 1)


def pack_kernel(vectors, amps, out):
    out[0] = vectors[...]
    wide = amps[...].astype(jnp.float32)
    for group in range(8):
        for slot in range(2):
            tile = wide[group * 8 : (group + 1) * 8, slot * 1024 : (slot + 1) * 1024]
            out[1, group * 2 + slot] = tile.astype(jnp.bfloat16)


def choose_vectors(orbitals, own, other, out):
    core = lax.axis_index("core")
    for dest in range(16):
        pair = pair_at(dest // 4, dest % 4, core)
        for side in range(2):
            for which, source in enumerate((own, other)):
                chosen = source[0, orbitals[side, pair]]
                for part in range(4):
                    out[dest, side * 8 + which * 4 + part] = chosen[:, part * 256 : (part + 1) * 256]


def hold_amps(own, other, held):
    core = lax.axis_index("core")
    held[core] = own[1]
    held[1 - core] = other[1]


def place_of(offsets, chip, pair):
    start, middle = offsets[chip * 2], offsets[chip * 2 + 1]
    late = pair >= middle
    return late.astype(jnp.int32), jnp.clip(jnp.where(late, pair - middle, pair - start), 0, 1)


def prepare_kernel(offsets, orbitals, own, other, out, held):
    choose_vectors(orbitals, own, other, out)
    hold_amps(own, other, held)
    chip = lax.axis_index("zl") * 4 + lax.axis_index("y")
    first = first_at(offsets, chip, lax.axis_index("core"))
    for kind in range(4):
        pair = first + 2 * jnp.minimum((kind - (first >> 1)) & 3, 1)
        late, slot = place_of(offsets, chip, pair)
        for y in range(4):
            for group in range(2):
                tile = held[late, (y * 2 + group) * 2 + slot]
                for part in range(4):
                    out[kind * 4 + y, 16 + group * 4 + part] = tile[:, part * 256 : (part + 1) * 256]


def tile_kernel(offsets, orbitals, own, other, out, tiles, held):
    choose_vectors(orbitals, own, other, out)
    hold_amps(own, other, held)
    chip = lax.axis_index("zl") * 4 + lax.axis_index("y")
    first = first_at(offsets, chip, lax.axis_index("core"))
    for j in range(2):
        late, slot = place_of(offsets, chip, first + 2 * j)
        for dest in range(16):
            tile = held[late, dest // 2 * 2 + slot]
            for part in range(2):
                start = dest % 2 * 512 + part * 256
                tiles[dest, j * 2 + part] = tile[:, start : start + 256]


def fill_kernel(offsets, chosen, tiles, token, local, out):
    out[:, :16] = chosen[...]
    core = lax.axis_index("core")
    for chip in range(16):
        for j in range(2):
            pair = first_at(offsets, chip, core) + 2 * j

            @pl.when(pair < offsets[chip * 2 + 2])
            def _():
                dest = ((pair & 7) >> 1) * 4 + (pair >> 3)
                for part in range(2):
                    out[dest, 16 + part] = tiles[chip, j * 2 + part]


def local_kernel(offsets, orbitals, energy, own, fock, after, out):
    owner = owner_index()
    tiles = [own[1, group * 2 + slot].astype(jnp.float32) for slot in range(2) for group in range(8)]
    both = jnp.concatenate(tiles, axis=0)
    term = jnp.dot(both.astype(jnp.bfloat16), fock[...], preferred_element_type=jnp.float32)
    for slot in range(2):
        pair = jnp.minimum(offsets[owner] + slot, 31)
        shift = energy[orbitals[0, pair]] + energy[orbitals[1, pair]]
        here = slice(slot * 64, (slot + 1) * 64)
        out[:, slot * 1024 : (slot + 1) * 1024] = term[here] - shift * both[here]


def chip_of(offsets, pair):
    chip = jnp.int32(0)
    for end in range(2, 32, 2):
        chip += (offsets[end] <= pair).astype(jnp.int32)
    return chip


def couple_kernel(offsets, case, arrived, out, rows, cols):
    zl, y, core = (lax.axis_index(name) for name in PAIR)
    swap = jnp.where(case[pair_at(zl, y, core)] == 0, 0.5, -0.5).astype(jnp.float32)
    for part in range(4):
        here = slice(part * 256, (part + 1) * 256)
        for which in range(2):
            left = arrived[:, which * 4 + part].astype(jnp.float32).reshape(128, 256)
            right = arrived[:, 8 + which * 4 + part].astype(jnp.float32).reshape(128, 256)
            start = which * 128
            rows[start : start + 128, here] = left
            rows[start + 256 : start + 384, here] = right
            cols[start : start + 128, here] = (0.5 * right).astype(jnp.bfloat16)
            cols[start + 256 : start + 384, here] = (swap * left).astype(jnp.bfloat16)
    for row in range(4):
        block = rows[:, row * 256 : (row + 1) * 256].T.astype(jnp.bfloat16)
        for part in range(4):
            there = cols[:, part * 256 : (part + 1) * 256]
            product = jnp.dot(block, there, preferred_element_type=jnp.float32)
            out[row * 4 + part, 0:256] = product.astype(jnp.bfloat16)
    for source in range(4):
        pair = pair_at(zl, source, core)
        chip = chip_of(offsets, pair)
        for part in range(4):
            tiles = [arrived[chip, 16 + group * 4 + part].astype(jnp.float32) for group in range(2)]
            tile = jnp.concatenate(tiles, axis=0).astype(jnp.bfloat16)
            for row in range(4):
                out[row * 4 + part, 256 + source * 16 : 272 + source * 16] = tile


def finish_kernel(parts, fock, out, cols):
    x, zh = lax.axis_index("x"), lax.axis_index("zh")
    cols[...] = jnp.zeros((512, 1024), jnp.bfloat16)
    for band in range(4):
        for quarter in range(4):
            start = pl.multiple_of(band * 128 + (zh & 1) * 64 + quarter * 16, 16)
            for y in range(4):
                tile = parts[band * 4 + quarter, 256 + y * 16 : 272 + y * 16]
                cols[pl.ds(start, 16), y * 256 : (y + 1) * 256] = tile
    top = pl.multiple_of(x * 256, 256)
    lanes = [pl.multiple_of((band * 2 + (zh >> 1)) * 128, 128) for band in range(4)]
    rows = jnp.concatenate([fock[pl.ds(top, 256), pl.ds(lane, 128)] for lane in lanes], axis=1)
    for y in range(4):
        total = jnp.dot(rows, cols[:, y * 256 : (y + 1) * 256], preferred_element_type=jnp.float32)
        for band in range(4):
            total += parts[band * 4 + y, 0:256].astype(jnp.float32)
        for dest in range(4):
            out[dest, y] = total[dest * 64 : (dest + 1) * 64].astype(jnp.bfloat16)


def late_couple_kernel(offsets, case, arrived, fock, out, rows, cols):
    zl = lax.axis_index("zl")
    pair = pair_at(zl, lax.axis_index("y"), lax.axis_index("core"))
    run = lax.axis_index("zh") + (zl >= 2).astype(jnp.int32)
    x, zh = lax.axis_index("x"), (run + 3 + (chip_of(offsets, pair) < 8).astype(jnp.int32)) & 3
    swap = jnp.where(case[pair] == 0, 0.5, -0.5).astype(jnp.float32)
    cols[512:640] = jnp.zeros((128, 1024), jnp.bfloat16)
    top = pl.multiple_of(512 + (zh & 1) * 64, 64)
    for part in range(4):
        here = slice(part * 256, (part + 1) * 256)
        for which in range(2):
            left = arrived[:, which * 4 + part].astype(jnp.float32).reshape(128, 256)
            right = arrived[:, 8 + which * 4 + part].astype(jnp.float32).reshape(128, 256)
            start = which * 128
            rows[start : start + 128, here] = left
            rows[start + 256 : start + 384, here] = right
            cols[start : start + 128, here] = (0.5 * right).astype(jnp.bfloat16)
            cols[start + 256 : start + 384, here] = (swap * left).astype(jnp.bfloat16)
        tiles = [arrived[group * 2 + part // 2, 16 + part % 2].astype(jnp.float32) for group in range(8)]
        cols[pl.ds(top, 64), here] = jnp.concatenate(tiles, axis=0).astype(jnp.bfloat16)
    lanes = pl.multiple_of((x * 2 + (zh >> 1)) * 128, 128)
    for row in range(4):
        here = slice(row * 256, (row + 1) * 256)
        block = jnp.concatenate([rows[:, here].T.astype(jnp.bfloat16), fock[here, pl.ds(lanes, 128)]], axis=1)
        product = jnp.dot(block, cols[...], preferred_element_type=jnp.float32)
        out[row] = product.astype(jnp.bfloat16)


def late_finish_kernel(parts, out):
    for y in range(4):
        here = slice(y * 256, (y + 1) * 256)
        total = parts[0, :, here].astype(jnp.float32)
        for x in range(1, 4):
            total += parts[x, :, here].astype(jnp.float32)
        for zh in range(4):
            out[zh * 4 + y] = total[zh * 64 : (zh + 1) * 64].astype(jnp.bfloat16)


def route_kernel(offsets, parts, out, total):
    for y in range(4):
        sums = parts[0, y].astype(jnp.float32)
        for zh in range(1, 4):
            sums += parts[zh, y].astype(jnp.float32)
        total[y] = sums.astype(jnp.bfloat16)
    member = lax.axis_index("zl") * 2 + lax.axis_index("core")
    for chip in range(16):
        end = offsets[chip * 2 + 2]
        which = jnp.maximum(((end + 7 - member) >> 3) - 1, 0)
        out[chip] = total[which]


def pick_kernel(offsets, arrived, mine, theirs):
    core, owner = lax.axis_index("core"), owner_index()
    for who, out in ((owner, mine), (owner ^ 1, theirs)):
        first = offsets[who]
        pair = first + ((first ^ core) & 1)
        for y in range(4):
            out[:, y * 256 : (y + 1) * 256] = arrived[((pair & 7) >> 1) * 4 + y]


def write_kernel(offsets, mine, other, local, out):
    owner = owner_index()
    first = offsets[owner]
    count = offsets[owner + 1] - first
    for slot in range(2):
        own = ((first + slot) & 1) == lax.axis_index("core")
        coupled = jnp.where(own, mine[...].astype(jnp.float32), other[...].astype(jnp.float32))
        result = coupled + local[:, slot * 1024 : (slot + 1) * 1024]
        out[:, slot, :] = jnp.where(slot < count, result, 0.0)


def call(kernel, out, in_specs, *args, scratch=()):
    return pl.pallas_call(
        kernel,
        out_shape=out,
        in_specs=in_specs,
        out_specs=jax.tree.map(lambda _: VMEM, out),
        scratch_shapes=list(scratch),
        compiler_params=LIMIT,
    )(*args)


def half(*shape):
    return jax.ShapeDtypeStruct(shape, jnp.bfloat16)


def single(*shape):
    return jax.ShapeDtypeStruct(shape, jnp.float32)


def shifted(block):
    runs = [[((run + (zl < 2)) % 4 * 4 + zl) * 4 + y for zl in range(4) for y in range(4)] for run in range(4)]
    return lax.all_to_all(block, ("zh", "zl", "y"), 0, 0, axis_index_groups=runs, tiled=True)


def local_part(own, fock, orbital_energy, orbitals, owner_offsets, after):
    return call(
        local_kernel, single(64, 2048), [SMEM] * 3 + [VMEM] * 2 + [ANY],
        owner_offsets, orbitals, orbital_energy, own, fock, after,
    )


def deliver(parts, owner_offsets):
    routed = call(
        route_kernel, half(16, 64, 256), [SMEM, VMEM], owner_offsets, parts,
        scratch=[pltpu.VMEM((4, 64, 256), jnp.bfloat16)],
    )
    arrived = lax.all_to_all(routed, ("zl", "y"), 0, 0, tiled=True)
    return call(pick_kernel, [half(64, 1024), half(64, 1024)], [SMEM, VMEM], owner_offsets, arrived)


def early_chain(own, other, fock, orbital_energy, orbitals, pair_case, owner_offsets):
    chosen = call(
        prepare_kernel, half(16, 24, 8, 256), [SMEM] * 2 + [VMEM] * 2, owner_offsets, orbitals, own, other,
        scratch=[pltpu.VMEM((2, 16, 8, 1024), jnp.bfloat16)],
    )
    arrived = lax.all_to_all(chosen, ("zl", "y"), 0, 0, tiled=True)
    partial = call(
        couple_kernel, half(16, 320, 256), [SMEM, SMEM, VMEM], owner_offsets, pair_case, arrived,
        scratch=[pltpu.VMEM((512, 1024), jnp.float32), pltpu.VMEM((512, 1024), jnp.bfloat16)],
    )
    parts = lax.all_to_all(partial, ("x", "y"), 0, 0, tiled=True)
    parts = call(
        finish_kernel, half(4, 4, 64, 256), [VMEM, VMEM], parts, fock, scratch=[pltpu.VMEM((512, 1024), jnp.bfloat16)]
    )
    parts = lax.all_to_all(parts, "zh", 0, 0, tiled=True)
    mine, theirs = deliver(parts, owner_offsets)
    local = local_part(own, fock, orbital_energy, orbitals, owner_offsets, mine)
    return mine, theirs, local


def late_chain(own, other, fock, orbital_energy, orbitals, pair_case, owner_offsets):
    chosen, tiles = call(
        tile_kernel, [half(16, 16, 8, 256), half(16, 4, 8, 256)], [SMEM] * 2 + [VMEM] * 2,
        owner_offsets, orbitals, own, other, scratch=[pltpu.VMEM((2, 16, 8, 1024), jnp.bfloat16)],
    )
    tiles = shifted(tiles)
    token = tiles[0, 0] if AFTER else other[0, 0, :, :128]
    for axis in TURNS:
        token = lax.ppermute(token, (axis, "core"), [(i * 2 + 1, (i + 1) % 4 * 2 + 1) for i in range(4)])
    local = local_part(own, fock, orbital_energy, orbitals, owner_offsets, tiles)
    chosen = call(
        fill_kernel, half(16, 18, 8, 256), [SMEM] + [VMEM] * 2 + [ANY] * 2, owner_offsets, chosen, tiles, token, local
    )
    arrived = shifted(chosen)
    partial = call(
        late_couple_kernel, half(4, 256, 1024), [SMEM, SMEM, VMEM, VMEM], owner_offsets, pair_case, arrived, fock,
        scratch=[pltpu.VMEM((512, 1024), jnp.float32), pltpu.VMEM((640, 1024), jnp.bfloat16)],
    )
    parts = lax.all_to_all(partial, "x", 0, 0, tiled=True)
    parts = call(late_finish_kernel, half(16, 64, 256), [VMEM], parts)
    parts = lax.all_to_all(parts, ("zh", "y"), 0, 0, tiled=True).reshape(4, 4, 64, 256)
    mine, theirs = deliver(parts, owner_offsets)
    return mine, theirs, local


def body(chol_vectors, amplitudes, fock, orbital_energy, pair_orbitals, pair_case, owner_offsets):
    flat = amplitudes.reshape(64, 2048)
    orbitals = pair_orbitals.T

    own = call(pack_kernel, half(2, 16, 8, 1024), [VMEM] * 2, chol_vectors, flat)
    other = lax.ppermute(own, "core", [(0, 1), (1, 0)])
    mine, theirs, local = lax.cond(
        lax.axis_index("core") == 0, early_chain, late_chain,
        own, other, fock, orbital_energy, orbitals, pair_case, owner_offsets,
    )
    other = lax.ppermute(theirs, "core", [(0, 1), (1, 0)])
    return call(write_kernel, single(64, 2, 1024), [SMEM] + [VMEM] * 3, owner_offsets, mine, other, local)


def solution(mesh):
    fine = Mesh(mesh.devices.reshape(4, 4, 4, 4, 2), ("x", "zh", "zl", "y", "core"))
    in_specs = (P(None, CHOL + PAIR, None), P(CHOL, PAIR, None), P(), P(), P(), P(), P())
    return jax.shard_map(body, mesh=fine, in_specs=in_specs, out_specs=P(CHOL, PAIR, None), check_vma=False)
```

```python
import jax
import jax.numpy as jnp
from jax import lax
from jax.experimental import pallas as pl
from jax.experimental.pallas import tpu as pltpu
from jax.sharding import Mesh, PartitionSpec as P

CHOL = ("x", "zh")
PAIR = ("zl", "y", "core")
VMEM = pl.BlockSpec(memory_space=pltpu.VMEM)
ANY = pl.BlockSpec(memory_space=pl.ANY)
TURNS = ("zh",)
SMEM = pl.BlockSpec(memory_space=pltpu.SMEM)
LIMIT = pltpu.CompilerParams(vmem_limit_bytes=32 * 1024 * 1024)


def pair_at(zl, y, core):
    return y * 8 + zl * 2 + core


def owner_index():
    return lax.axis_index("zl") * 8 + lax.axis_index("y") * 2 + lax.axis_index("core")


def first_at(offsets, chip, core):
    first = offsets[chip * 2]
    return first + ((first ^ core) & 1)


def pack_kernel(vectors, amps, out):
    out[0] = vectors[...]
    wide = amps[...].astype(jnp.float32)
    for group in range(8):
        for slot in range(2):
            tile = wide[group * 8 : (group + 1) * 8, slot * 1024 : (slot + 1) * 1024]
            out[1, group * 2 + slot] = tile.astype(jnp.bfloat16)


def choose_vectors(orbitals, own, other, out):
    core = lax.axis_index("core")
    for dest in range(16):
        pair = pair_at(dest // 4, dest % 4, core)
        for side in range(2):
            for which, source in enumerate((own, other)):
                chosen = source[0, orbitals[side, pair]]
                for part in range(4):
                    out[dest, side * 8 + which * 4 + part] = chosen[:, part * 256 : (part + 1) * 256]


def hold_amps(own, other, held):
    core = lax.axis_index("core")
    held[core] = own[1]
    held[1 - core] = other[1]


def place_of(offsets, chip, pair):
    start, middle = offsets[chip * 2], offsets[chip * 2 + 1]
    late = pair >= middle
    return late.astype(jnp.int32), jnp.clip(jnp.where(late, pair - middle, pair - start), 0, 1)


def prepare_kernel(offsets, orbitals, own, other, out, held):
    choose_vectors(orbitals, own, other, out)
    hold_amps(own, other, held)
    chip = lax.axis_index("zl") * 4 + lax.axis_index("y")
    first = first_at(offsets, chip, lax.axis_index("core"))
    for kind in range(4):
        pair = first + 2 * jnp.minimum((kind - (first >> 1)) & 3, 1)
        late, slot = place_of(offsets, chip, pair)
        for y in range(4):
            for group in range(2):
                tile = held[late, (y * 2 + group) * 2 + slot]
                for part in range(4):
                    out[kind * 4 + y, 16 + group * 4 + part] = tile[:, part * 256 : (part + 1) * 256]


def tile_kernel(offsets, orbitals, own, other, out, tiles, held):
    choose_vectors(orbitals, own, other, out)
    hold_amps(own, other, held)
    chip = lax.axis_index("zl") * 4 + lax.axis_index("y")
    first = first_at(offsets, chip, lax.axis_index("core"))
    for j in range(2):
        late, slot = place_of(offsets, chip, first + 2 * j)
        for dest in range(16):
            tile = held[late, dest // 2 * 2 + slot]
            for part in range(2):
                start = dest % 2 * 512 + part * 256
                tiles[dest, j * 2 + part] = tile[:, start : start + 256]


def fill_kernel(offsets, chosen, tiles, token, local, out):
    out[:, :16] = chosen[...]
    core = lax.axis_index("core")
    for chip in range(16):
        for j in range(2):
            pair = first_at(offsets, chip, core) + 2 * j

            @pl.when(pair < offsets[chip * 2 + 2])
            def _():
                dest = ((pair & 7) >> 1) * 4 + (pair >> 3)
                for part in range(2):
                    out[dest, 16 + part] = tiles[chip, j * 2 + part]


def local_kernel(offsets, orbitals, energy, own, fock, after, out):
    owner = owner_index()
    tiles = [own[1, group * 2 + slot].astype(jnp.float32) for slot in range(2) for group in range(8)]
    both = jnp.concatenate(tiles, axis=0)
    term = jnp.dot(both.astype(jnp.bfloat16), fock[...], preferred_element_type=jnp.float32)
    for slot in range(2):
        pair = jnp.minimum(offsets[owner] + slot, 31)
        shift = energy[orbitals[0, pair]] + energy[orbitals[1, pair]]
        here = slice(slot * 64, (slot + 1) * 64)
        out[:, slot * 1024 : (slot + 1) * 1024] = term[here] - shift * both[here]


def chip_of(offsets, pair):
    chip = jnp.int32(0)
    for end in range(2, 32, 2):
        chip += (offsets[end] <= pair).astype(jnp.int32)
    return chip


def couple_kernel(offsets, case, arrived, out, rows, cols):
    zl, y, core = (lax.axis_index(name) for name in PAIR)
    swap = jnp.where(case[pair_at(zl, y, core)] == 0, 0.5, -0.5).astype(jnp.float32)
    for part in range(4):
        here = slice(part * 256, (part + 1) * 256)
        for which in range(2):
            left = arrived[:, which * 4 + part].astype(jnp.float32).reshape(128, 256)
            right = arrived[:, 8 + which * 4 + part].astype(jnp.float32).reshape(128, 256)
            start = which * 128
            rows[start : start + 128, here] = left
            rows[start + 256 : start + 384, here] = right
            cols[start : start + 128, here] = (0.5 * right).astype(jnp.bfloat16)
            cols[start + 256 : start + 384, here] = (swap * left).astype(jnp.bfloat16)
    for row in range(4):
        block = rows[:, row * 256 : (row + 1) * 256].T.astype(jnp.bfloat16)
        for part in range(4):
            there = cols[:, part * 256 : (part + 1) * 256]
            product = jnp.dot(block, there, preferred_element_type=jnp.float32)
            out[row * 4 + part, 0:256] = product.astype(jnp.bfloat16)
    for source in range(4):
        pair = pair_at(zl, source, core)
        chip = chip_of(offsets, pair)
        for part in range(4):
            tiles = [arrived[chip, 16 + group * 4 + part].astype(jnp.float32) for group in range(2)]
            tile = jnp.concatenate(tiles, axis=0).astype(jnp.bfloat16)
            for row in range(4):
                out[row * 4 + part, 256 + source * 16 : 272 + source * 16] = tile


def finish_kernel(parts, fock, out, cols):
    x, zh = lax.axis_index("x"), lax.axis_index("zh")
    cols[...] = jnp.zeros((512, 1024), jnp.bfloat16)
    for band in range(4):
        for quarter in range(4):
            start = pl.multiple_of(band * 128 + (zh & 1) * 64 + quarter * 16, 16)
            for y in range(4):
                tile = parts[band * 4 + quarter, 256 + y * 16 : 272 + y * 16]
                cols[pl.ds(start, 16), y * 256 : (y + 1) * 256] = tile
    top = pl.multiple_of(x * 256, 256)
    lanes = [pl.multiple_of((band * 2 + (zh >> 1)) * 128, 128) for band in range(4)]
    rows = jnp.concatenate([fock[pl.ds(top, 256), pl.ds(lane, 128)] for lane in lanes], axis=1)
    for y in range(4):
        total = jnp.dot(rows, cols[:, y * 256 : (y + 1) * 256], preferred_element_type=jnp.float32)
        for band in range(4):
            total += parts[band * 4 + y, 0:256].astype(jnp.float32)
        for dest in range(4):
            out[dest, y] = total[dest * 64 : (dest + 1) * 64].astype(jnp.bfloat16)


def late_couple_kernel(offsets, case, arrived, fock, out, rows, cols):
    zl = lax.axis_index("zl")
    pair = pair_at(zl, lax.axis_index("y"), lax.axis_index("core"))
    run = lax.axis_index("zh") + (zl >= 2).astype(jnp.int32)
    x, zh = lax.axis_index("x"), (run + 3 + (chip_of(offsets, pair) < 8).astype(jnp.int32)) & 3
    swap = jnp.where(case[pair] == 0, 0.5, -0.5).astype(jnp.float32)
    cols[512:640] = jnp.zeros((128, 1024), jnp.bfloat16)
    top = pl.multiple_of(512 + (zh & 1) * 64, 64)
    for part in range(4):
        here = slice(part * 256, (part + 1) * 256)
        for which in range(2):
            left = arrived[:, which * 4 + part].astype(jnp.float32).reshape(128, 256)
            right = arrived[:, 8 + which * 4 + part].astype(jnp.float32).reshape(128, 256)
            start = which * 128
            rows[start : start + 128, here] = left
            rows[start + 256 : start + 384, here] = right
            cols[start : start + 128, here] = (0.5 * right).astype(jnp.bfloat16)
            cols[start + 256 : start + 384, here] = (swap * left).astype(jnp.bfloat16)
        tiles = [arrived[group * 2 + part // 2, 16 + part % 2].astype(jnp.float32) for group in range(8)]
        cols[pl.ds(top, 64), here] = jnp.concatenate(tiles, axis=0).astype(jnp.bfloat16)
    lanes = pl.multiple_of((x * 2 + (zh >> 1)) * 128, 128)
    for row in range(4):
        here = slice(row * 256, (row + 1) * 256)
        block = jnp.concatenate([rows[:, here].T.astype(jnp.bfloat16), fock[here, pl.ds(lanes, 128)]], axis=1)
        product = jnp.dot(block, cols[...], preferred_element_type=jnp.float32)
        out[row] = product.astype(jnp.bfloat16)


def late_finish_kernel(parts, out):
    for y in range(4):
        here = slice(y * 256, (y + 1) * 256)
        total = parts[0, :, here].astype(jnp.float32)
        for x in range(1, 4):
            total += parts[x, :, here].astype(jnp.float32)
        for zh in range(4):
            out[zh * 4 + y] = total[zh * 64 : (zh + 1) * 64].astype(jnp.bfloat16)


def route_kernel(offsets, parts, out, total):
    for y in range(4):
        sums = parts[0, y].astype(jnp.float32)
        for zh in range(1, 4):
            sums += parts[zh, y].astype(jnp.float32)
        total[y] = sums.astype(jnp.bfloat16)
    member = lax.axis_index("zl") * 2 + lax.axis_index("core")
    for chip in range(16):
        end = offsets[chip * 2 + 2]
        which = jnp.maximum(((end + 7 - member) >> 3) - 1, 0)
        out[chip] = total[which]


def pick_kernel(offsets, arrived, mine, theirs):
    core, owner = lax.axis_index("core"), owner_index()
    for who, out in ((owner, mine), (owner ^ 1, theirs)):
        first = offsets[who]
        pair = first + ((first ^ core) & 1)
        for y in range(4):
            out[:, y * 256 : (y + 1) * 256] = arrived[((pair & 7) >> 1) * 4 + y]


def write_kernel(offsets, mine, other, local, out):
    owner = owner_index()
    first = offsets[owner]
    count = offsets[owner + 1] - first
    for slot in range(2):
        own = ((first + slot) & 1) == lax.axis_index("core")
        coupled = jnp.where(own, mine[...].astype(jnp.float32), other[...].astype(jnp.float32))
        result = coupled + local[:, slot * 1024 : (slot + 1) * 1024]
        out[:, slot, :] = jnp.where(slot < count, result, 0.0)


def call(kernel, out, in_specs, *args, scratch=()):
    return pl.pallas_call(
        kernel,
        out_shape=out,
        in_specs=in_specs,
        out_specs=jax.tree.map(lambda _: VMEM, out),
        scratch_shapes=list(scratch),
        compiler_params=LIMIT,
    )(*args)


def half(*shape):
    return jax.ShapeDtypeStruct(shape, jnp.bfloat16)


def single(*shape):
    return jax.ShapeDtypeStruct(shape, jnp.float32)


def shifted(block):
    runs = [[((run + (zl < 2)) % 4 * 4 + zl) * 4 + y for zl in range(4) for y in range(4)] for run in range(4)]
    return lax.all_to_all(block, ("zh", "zl", "y"), 0, 0, axis_index_groups=runs, tiled=True)


def local_part(own, fock, orbital_energy, orbitals, owner_offsets, after):
    return call(
        local_kernel, single(64, 2048), [SMEM] * 3 + [VMEM] * 2 + [ANY],
        owner_offsets, orbitals, orbital_energy, own, fock, after,
    )


def deliver(parts, owner_offsets):
    routed = call(
        route_kernel, half(16, 64, 256), [SMEM, VMEM], owner_offsets, parts,
        scratch=[pltpu.VMEM((4, 64, 256), jnp.bfloat16)],
    )
    arrived = lax.all_to_all(routed, ("zl", "y"), 0, 0, tiled=True)
    return call(pick_kernel, [half(64, 1024), half(64, 1024)], [SMEM, VMEM], owner_offsets, arrived)


def early_chain(own, other, fock, orbital_energy, orbitals, pair_case, owner_offsets):
    chosen = call(
        prepare_kernel, half(16, 24, 8, 256), [SMEM] * 2 + [VMEM] * 2, owner_offsets, orbitals, own, other,
        scratch=[pltpu.VMEM((2, 16, 8, 1024), jnp.bfloat16)],
    )
    arrived = lax.all_to_all(chosen, ("zl", "y"), 0, 0, tiled=True)
    partial = call(
        couple_kernel, half(16, 320, 256), [SMEM, SMEM, VMEM], owner_offsets, pair_case, arrived,
        scratch=[pltpu.VMEM((512, 1024), jnp.float32), pltpu.VMEM((512, 1024), jnp.bfloat16)],
    )
    parts = lax.all_to_all(partial, ("x", "y"), 0, 0, tiled=True)
    parts = call(
        finish_kernel, half(4, 4, 64, 256), [VMEM, VMEM], parts, fock, scratch=[pltpu.VMEM((512, 1024), jnp.bfloat16)]
    )
    parts = lax.all_to_all(parts, "zh", 0, 0, tiled=True)
    return parts, local_part(own, fock, orbital_energy, orbitals, owner_offsets, parts)


def late_chain(own, other, fock, orbital_energy, orbitals, pair_case, owner_offsets):
    chosen, tiles = call(
        tile_kernel, [half(16, 16, 8, 256), half(16, 4, 8, 256)], [SMEM] * 2 + [VMEM] * 2,
        owner_offsets, orbitals, own, other, scratch=[pltpu.VMEM((2, 16, 8, 1024), jnp.bfloat16)],
    )
    tiles = shifted(tiles)
    token = other[0, 0, :, :128]
    for axis in TURNS:
        token = lax.ppermute(token, (axis, "core"), [(i * 2 + 1, (i + 1) % 4 * 2 + 1) for i in range(4)])
    local = local_part(own, fock, orbital_energy, orbitals, owner_offsets, tiles)
    chosen = call(
        fill_kernel, half(16, 18, 8, 256), [SMEM] + [VMEM] * 2 + [ANY] * 2, owner_offsets, chosen, tiles, token, local
    )
    arrived = shifted(chosen)
    partial = call(
        late_couple_kernel, half(4, 256, 1024), [SMEM, SMEM, VMEM, VMEM], owner_offsets, pair_case, arrived, fock,
        scratch=[pltpu.VMEM((512, 1024), jnp.float32), pltpu.VMEM((640, 1024), jnp.bfloat16)],
    )
    parts = lax.all_to_all(partial, "x", 0, 0, tiled=True)
    parts = call(late_finish_kernel, half(16, 64, 256), [VMEM], parts)
    parts = lax.all_to_all(parts, ("zh", "y"), 0, 0, tiled=True).reshape(4, 4, 64, 256)
    return parts, local


def body(chol_vectors, amplitudes, fock, orbital_energy, pair_orbitals, pair_case, owner_offsets):
    flat = amplitudes.reshape(64, 2048)
    orbitals = pair_orbitals.T

    own = call(pack_kernel, half(2, 16, 8, 1024), [VMEM] * 2, chol_vectors, flat)
    other = lax.ppermute(own, "core", [(0, 1), (1, 0)])
    parts, local = lax.cond(
        lax.axis_index("core") == 0, early_chain, late_chain,
        own, other, fock, orbital_energy, orbitals, pair_case, owner_offsets,
    )
    mine, theirs = deliver(parts, owner_offsets)
    other = lax.ppermute(theirs, "core", [(0, 1), (1, 0)])
    return call(write_kernel, single(64, 2, 1024), [SMEM] + [VMEM] * 3, owner_offsets, mine, other, local)


def solution(mesh):
    fine = Mesh(mesh.devices.reshape(4, 4, 4, 4, 2), ("x", "zh", "zl", "y", "core"))
    in_specs = (P(None, CHOL + PAIR, None), P(CHOL, PAIR, None), P(), P(), P(), P(), P())
    return jax.shard_map(body, mesh=fine, in_specs=in_specs, out_specs=P(CHOL, PAIR, None), check_vma=False)
```

```python
import jax
import jax.numpy as jnp
from jax import lax
from jax.experimental import pallas as pl
from jax.experimental.pallas import tpu as pltpu
from jax.sharding import Mesh, PartitionSpec as P

CHOL = ("x", "zh")
PAIR = ("zl", "y", "core")
VMEM = pl.BlockSpec(memory_space=pltpu.VMEM)
ANY = pl.BlockSpec(memory_space=pl.ANY)
TURNS = ("zh",)
SMEM = pl.BlockSpec(memory_space=pltpu.SMEM)
LIMIT = pltpu.CompilerParams(vmem_limit_bytes=32 * 1024 * 1024)


def pair_at(zl, y, core):
    return y * 8 + zl * 2 + core


def owner_index():
    return lax.axis_index("zl") * 8 + lax.axis_index("y") * 2 + lax.axis_index("core")


def first_at(offsets, chip, core):
    first = offsets[chip * 2]
    return first + ((first ^ core) & 1)


def pack_kernel(vectors, amps, out):
    out[0] = vectors[...]
    wide = amps[...].astype(jnp.float32)
    for group in range(8):
        for slot in range(2):
            tile = wide[group * 8 : (group + 1) * 8, slot * 1024 : (slot + 1) * 1024]
            out[1, group * 2 + slot] = tile.astype(jnp.bfloat16)


def choose_vectors(orbitals, own, other, out):
    core = lax.axis_index("core")
    for dest in range(16):
        pair = pair_at(dest // 4, dest % 4, core)
        for side in range(2):
            for which, source in enumerate((own, other)):
                chosen = source[0, orbitals[side, pair]]
                for part in range(4):
                    out[dest, side * 8 + which * 4 + part] = chosen[:, part * 256 : (part + 1) * 256]


def hold_amps(own, other, held):
    core = lax.axis_index("core")
    held[core] = own[1]
    held[1 - core] = other[1]


def place_of(offsets, chip, pair):
    start, middle = offsets[chip * 2], offsets[chip * 2 + 1]
    late = pair >= middle
    return late.astype(jnp.int32), jnp.clip(jnp.where(late, pair - middle, pair - start), 0, 1)


def prepare_kernel(offsets, orbitals, own, other, out, held):
    choose_vectors(orbitals, own, other, out)
    hold_amps(own, other, held)
    chip = lax.axis_index("zl") * 4 + lax.axis_index("y")
    first = first_at(offsets, chip, lax.axis_index("core"))
    for kind in range(4):
        pair = first + 2 * jnp.minimum((kind - (first >> 1)) & 3, 1)
        late, slot = place_of(offsets, chip, pair)
        for y in range(4):
            for group in range(2):
                tile = held[late, (y * 2 + group) * 2 + slot]
                for part in range(4):
                    out[kind * 4 + y, 16 + group * 4 + part] = tile[:, part * 256 : (part + 1) * 256]


def tile_kernel(offsets, orbitals, own, other, out, tiles, held):
    choose_vectors(orbitals, own, other, out)
    hold_amps(own, other, held)
    chip = lax.axis_index("zl") * 4 + lax.axis_index("y")
    first = first_at(offsets, chip, lax.axis_index("core"))
    for j in range(2):
        late, slot = place_of(offsets, chip, first + 2 * j)
        for dest in range(16):
            tile = held[late, dest // 2 * 2 + slot]
            for part in range(2):
                start = dest % 2 * 512 + part * 256
                tiles[dest, j * 2 + part] = tile[:, start : start + 256]


def fill_kernel(offsets, chosen, tiles, token, local, out):
    out[:, :16] = chosen[...]
    core = lax.axis_index("core")
    for chip in range(16):
        for j in range(2):
            pair = first_at(offsets, chip, core) + 2 * j

            @pl.when(pair < offsets[chip * 2 + 2])
            def _():
                dest = ((pair & 7) >> 1) * 4 + (pair >> 3)
                for part in range(2):
                    out[dest, 16 + part] = tiles[chip, j * 2 + part]


def local_kernel(offsets, orbitals, energy, own, fock, after, out):
    owner = owner_index()
    tiles = [own[1, group * 2 + slot].astype(jnp.float32) for slot in range(2) for group in range(8)]
    both = jnp.concatenate(tiles, axis=0)
    term = jnp.dot(both.astype(jnp.bfloat16), fock[...], preferred_element_type=jnp.float32)
    for slot in range(2):
        pair = jnp.minimum(offsets[owner] + slot, 31)
        shift = energy[orbitals[0, pair]] + energy[orbitals[1, pair]]
        here = slice(slot * 64, (slot + 1) * 64)
        out[:, slot * 1024 : (slot + 1) * 1024] = term[here] - shift * both[here]


def chip_of(offsets, pair):
    chip = jnp.int32(0)
    for end in range(2, 32, 2):
        chip += (offsets[end] <= pair).astype(jnp.int32)
    return chip


def couple_kernel(offsets, case, arrived, out, rows, cols):
    zl, y, core = (lax.axis_index(name) for name in PAIR)
    swap = jnp.where(case[pair_at(zl, y, core)] == 0, 0.5, -0.5).astype(jnp.float32)
    for part in range(4):
        here = slice(part * 256, (part + 1) * 256)
        for which in range(2):
            left = arrived[:, which * 4 + part].astype(jnp.float32).reshape(128, 256)
            right = arrived[:, 8 + which * 4 + part].astype(jnp.float32).reshape(128, 256)
            start = which * 128
            rows[start : start + 128, here] = left
            rows[start + 256 : start + 384, here] = right
            cols[start : start + 128, here] = (0.5 * right).astype(jnp.bfloat16)
            cols[start + 256 : start + 384, here] = (swap * left).astype(jnp.bfloat16)
    for row in range(4):
        block = rows[:, row * 256 : (row + 1) * 256].T.astype(jnp.bfloat16)
        for part in range(4):
            there = cols[:, part * 256 : (part + 1) * 256]
            product = jnp.dot(block, there, preferred_element_type=jnp.float32)
            out[row * 4 + part, 0:256] = product.astype(jnp.bfloat16)
    for source in range(4):
        pair = pair_at(zl, source, core)
        chip = chip_of(offsets, pair)
        for part in range(4):
            tiles = [arrived[chip, 16 + group * 4 + part].astype(jnp.float32) for group in range(2)]
            tile = jnp.concatenate(tiles, axis=0).astype(jnp.bfloat16)
            for row in range(4):
                out[row * 4 + part, 256 + source * 16 : 272 + source * 16] = tile


def finish_kernel(parts, fock, out, cols):
    x, zh = lax.axis_index("x"), lax.axis_index("zh")
    cols[...] = jnp.zeros((512, 1024), jnp.bfloat16)
    for band in range(4):
        for quarter in range(4):
            start = pl.multiple_of(band * 128 + (zh & 1) * 64 + quarter * 16, 16)
            for y in range(4):
                tile = parts[band * 4 + quarter, 256 + y * 16 : 272 + y * 16]
                cols[pl.ds(start, 16), y * 256 : (y + 1) * 256] = tile
    top = pl.multiple_of(x * 256, 256)
    lanes = [pl.multiple_of((band * 2 + (zh >> 1)) * 128, 128) for band in range(4)]
    rows = jnp.concatenate([fock[pl.ds(top, 256), pl.ds(lane, 128)] for lane in lanes], axis=1)
    for y in range(4):
        total = jnp.dot(rows, cols[:, y * 256 : (y + 1) * 256], preferred_element_type=jnp.float32)
        for band in range(4):
            total += parts[band * 4 + y, 0:256].astype(jnp.float32)
        for dest in range(4):
            out[dest, y] = total[dest * 64 : (dest + 1) * 64].astype(jnp.bfloat16)


def late_couple_kernel(offsets, case, arrived, fock, out, rows, cols):
    zl = lax.axis_index("zl")
    pair = pair_at(zl, lax.axis_index("y"), lax.axis_index("core"))
    run = lax.axis_index("zh") + (zl >= 2).astype(jnp.int32)
    x, zh = lax.axis_index("x"), (run + 3 + (chip_of(offsets, pair) < 8).astype(jnp.int32)) & 3
    swap = jnp.where(case[pair] == 0, 0.5, -0.5).astype(jnp.float32)
    cols[512:640] = jnp.zeros((128, 1024), jnp.bfloat16)
    top = pl.multiple_of(512 + (zh & 1) * 64, 64)
    for part in range(4):
        here = slice(part * 256, (part + 1) * 256)
        for which in range(2):
            left = arrived[:, which * 4 + part].astype(jnp.float32).reshape(128, 256)
            right = arrived[:, 8 + which * 4 + part].astype(jnp.float32).reshape(128, 256)
            start = which * 128
            rows[start : start + 128, here] = left
            rows[start + 256 : start + 384, here] = right
            cols[start : start + 128, here] = (0.5 * right).astype(jnp.bfloat16)
            cols[start + 256 : start + 384, here] = (swap * left).astype(jnp.bfloat16)
        tiles = [arrived[group * 2 + part // 2, 16 + part % 2].astype(jnp.float32) for group in range(8)]
        cols[pl.ds(top, 64), here] = jnp.concatenate(tiles, axis=0).astype(jnp.bfloat16)
    lanes = pl.multiple_of((x * 2 + (zh >> 1)) * 128, 128)
    for row in range(4):
        here = slice(row * 256, (row + 1) * 256)
        block = jnp.concatenate([rows[:, here].T.astype(jnp.bfloat16), fock[here, pl.ds(lanes, 128)]], axis=1)
        product = jnp.dot(block, cols[...], preferred_element_type=jnp.float32)
        out[row] = product.astype(jnp.bfloat16)


def late_finish_kernel(parts, out):
    for y in range(4):
        here = slice(y * 256, (y + 1) * 256)
        total = parts[0, :, here].astype(jnp.float32)
        for x in range(1, 4):
            total += parts[x, :, here].astype(jnp.float32)
        for zh in range(4):
            out[zh * 4 + y] = total[zh * 64 : (zh + 1) * 64].astype(jnp.bfloat16)


def route_kernel(offsets, parts, out, total):
    for y in range(4):
        sums = parts[0, y].astype(jnp.float32)
        for zh in range(1, 4):
            sums += parts[zh, y].astype(jnp.float32)
        total[y] = sums.astype(jnp.bfloat16)
    member = lax.axis_index("zl") * 2 + lax.axis_index("core")
    for chip in range(16):
        end = offsets[chip * 2 + 2]
        which = jnp.maximum(((end + 7 - member) >> 3) - 1, 0)
        out[chip] = total[which]


def pick_kernel(offsets, arrived, mine, theirs):
    core, owner = lax.axis_index("core"), owner_index()
    for who, out in ((owner, mine), (owner ^ 1, theirs)):
        first = offsets[who]
        pair = first + ((first ^ core) & 1)
        for y in range(4):
            out[:, y * 256 : (y + 1) * 256] = arrived[((pair & 7) >> 1) * 4 + y]


def write_kernel(offsets, mine, other, local, out):
    owner = owner_index()
    first = offsets[owner]
    count = offsets[owner + 1] - first
    for slot in range(2):
        own = ((first + slot) & 1) == lax.axis_index("core")
        coupled = jnp.where(own, mine[...].astype(jnp.float32), other[...].astype(jnp.float32))
        result = coupled + local[:, slot * 1024 : (slot + 1) * 1024]
        out[:, slot, :] = jnp.where(slot < count, result, 0.0)


def call(kernel, out, in_specs, *args, scratch=()):
    return pl.pallas_call(
        kernel,
        out_shape=out,
        in_specs=in_specs,
        out_specs=jax.tree.map(lambda _: VMEM, out),
        scratch_shapes=list(scratch),
        compiler_params=LIMIT,
    )(*args)


def half(*shape):
    return jax.ShapeDtypeStruct(shape, jnp.bfloat16)


def single(*shape):
    return jax.ShapeDtypeStruct(shape, jnp.float32)


def shifted(block):
    runs = [[((run + (zl < 2)) % 4 * 4 + zl) * 4 + y for zl in range(4) for y in range(4)] for run in range(4)]
    return lax.all_to_all(block, ("zh", "zl", "y"), 0, 0, axis_index_groups=runs, tiled=True)


def local_part(own, fock, orbital_energy, orbitals, owner_offsets, after):
    return call(
        local_kernel, single(64, 2048), [SMEM] * 3 + [VMEM] * 2 + [ANY],
        owner_offsets, orbitals, orbital_energy, own, fock, after,
    )


def route(parts, owner_offsets):
    return call(
        route_kernel, half(16, 64, 256), [SMEM, VMEM], owner_offsets, parts,
        scratch=[pltpu.VMEM((4, 64, 256), jnp.bfloat16)],
    )


def early_chain(own, other, fock, orbital_energy, orbitals, pair_case, owner_offsets):
    chosen = call(
        prepare_kernel, half(16, 24, 8, 256), [SMEM] * 2 + [VMEM] * 2, owner_offsets, orbitals, own, other,
        scratch=[pltpu.VMEM((2, 16, 8, 1024), jnp.bfloat16)],
    )
    arrived = lax.all_to_all(chosen, ("zl", "y"), 0, 0, tiled=True)
    partial = call(
        couple_kernel, half(16, 320, 256), [SMEM, SMEM, VMEM], owner_offsets, pair_case, arrived,
        scratch=[pltpu.VMEM((512, 1024), jnp.float32), pltpu.VMEM((512, 1024), jnp.bfloat16)],
    )
    parts = lax.all_to_all(partial, ("x", "y"), 0, 0, tiled=True)
    parts = call(
        finish_kernel, half(4, 4, 64, 256), [VMEM, VMEM], parts, fock, scratch=[pltpu.VMEM((512, 1024), jnp.bfloat16)]
    )
    parts = lax.all_to_all(parts, "zh", 0, 0, tiled=True)
    return route(parts, owner_offsets), local_part(own, fock, orbital_energy, orbitals, owner_offsets, parts)


def late_chain(own, other, fock, orbital_energy, orbitals, pair_case, owner_offsets):
    chosen, tiles = call(
        tile_kernel, [half(16, 16, 8, 256), half(16, 4, 8, 256)], [SMEM] * 2 + [VMEM] * 2,
        owner_offsets, orbitals, own, other, scratch=[pltpu.VMEM((2, 16, 8, 1024), jnp.bfloat16)],
    )
    tiles = shifted(tiles)
    token = other[0, 0, :, :128]
    for axis in TURNS:
        token = lax.ppermute(token, (axis, "core"), [(i * 2 + 1, (i + 1) % 4 * 2 + 1) for i in range(4)])
    local = local_part(own, fock, orbital_energy, orbitals, owner_offsets, tiles)
    chosen = call(
        fill_kernel, half(16, 18, 8, 256), [SMEM] + [VMEM] * 2 + [ANY] * 2, owner_offsets, chosen, tiles, token, local
    )
    arrived = shifted(chosen)
    partial = call(
        late_couple_kernel, half(4, 256, 1024), [SMEM, SMEM, VMEM, VMEM], owner_offsets, pair_case, arrived, fock,
        scratch=[pltpu.VMEM((512, 1024), jnp.float32), pltpu.VMEM((640, 1024), jnp.bfloat16)],
    )
    parts = lax.all_to_all(partial, "x", 0, 0, tiled=True)
    parts = call(late_finish_kernel, half(16, 64, 256), [VMEM], parts)
    parts = lax.all_to_all(parts, ("zh", "y"), 0, 0, tiled=True).reshape(4, 4, 64, 256)
    return route(parts, owner_offsets), local


def body(chol_vectors, amplitudes, fock, orbital_energy, pair_orbitals, pair_case, owner_offsets):
    flat = amplitudes.reshape(64, 2048)
    orbitals = pair_orbitals.T

    own = call(pack_kernel, half(2, 16, 8, 1024), [VMEM] * 2, chol_vectors, flat)
    other = lax.ppermute(own, "core", [(0, 1), (1, 0)])
    routed, local = lax.cond(
        lax.axis_index("core") == 0, early_chain, late_chain,
        own, other, fock, orbital_energy, orbitals, pair_case, owner_offsets,
    )
    arrived = lax.all_to_all(routed, ("zl", "y"), 0, 0, tiled=True)
    mine, theirs = call(pick_kernel, [half(64, 1024), half(64, 1024)], [SMEM, VMEM], owner_offsets, arrived)
    other = lax.ppermute(theirs, "core", [(0, 1), (1, 0)])
    return call(write_kernel, single(64, 2, 1024), [SMEM] + [VMEM] * 3, owner_offsets, mine, other, local)


def solution(mesh):
    fine = Mesh(mesh.devices.reshape(4, 4, 4, 4, 2), ("x", "zh", "zl", "y", "core"))
    in_specs = (P(None, CHOL + PAIR, None), P(CHOL, PAIR, None), P(), P(), P(), P(), P())
    return jax.shard_map(body, mesh=fine, in_specs=in_specs, out_specs=P(CHOL, PAIR, None), check_vma=False)
```

```python
import jax
import jax.numpy as jnp
from jax import lax
from jax.experimental import pallas as pl
from jax.experimental.pallas import tpu as pltpu
from jax.sharding import Mesh, PartitionSpec as P

CHOL = ("x", "zh")
PAIR = ("zl", "y", "core")
VMEM = pl.BlockSpec(memory_space=pltpu.VMEM)
ANY = pl.BlockSpec(memory_space=pl.ANY)
TURNS = ("zh",)
SMEM = pl.BlockSpec(memory_space=pltpu.SMEM)
LIMIT = pltpu.CompilerParams(vmem_limit_bytes=32 * 1024 * 1024)


def pair_at(zl, y, core):
    return y * 8 + zl * 2 + core


def owner_index():
    return lax.axis_index("zl") * 8 + lax.axis_index("y") * 2 + lax.axis_index("core")


def first_at(offsets, chip, core):
    first = offsets[chip * 2]
    return first + ((first ^ core) & 1)


def pack_kernel(vectors, amps, out):
    out[0] = vectors[...]
    wide = amps[...].astype(jnp.float32)
    for group in range(8):
        for slot in range(2):
            tile = wide[group * 8 : (group + 1) * 8, slot * 1024 : (slot + 1) * 1024]
            out[1, group * 2 + slot] = tile.astype(jnp.bfloat16)


def choose_vectors(orbitals, own, other, out):
    core = lax.axis_index("core")
    for dest in range(16):
        pair = pair_at(dest // 4, dest % 4, core)
        for side in range(2):
            for which, source in enumerate((own, other)):
                chosen = source[0, orbitals[side, pair]]
                for part in range(4):
                    out[dest, side * 8 + which * 4 + part] = chosen[:, part * 256 : (part + 1) * 256]


def hold_amps(own, other, held):
    core = lax.axis_index("core")
    held[core] = own[1]
    held[1 - core] = other[1]


def place_of(offsets, chip, pair):
    start, middle = offsets[chip * 2], offsets[chip * 2 + 1]
    late = pair >= middle
    return late.astype(jnp.int32), jnp.clip(jnp.where(late, pair - middle, pair - start), 0, 1)


def prepare_kernel(offsets, orbitals, own, other, out, held):
    choose_vectors(orbitals, own, other, out)
    hold_amps(own, other, held)
    chip = lax.axis_index("zl") * 4 + lax.axis_index("y")
    first = first_at(offsets, chip, lax.axis_index("core"))
    for kind in range(4):
        pair = first + 2 * jnp.minimum((kind - (first >> 1)) & 3, 1)
        late, slot = place_of(offsets, chip, pair)
        for y in range(4):
            for group in range(2):
                tile = held[late, (y * 2 + group) * 2 + slot]
                for part in range(4):
                    out[kind * 4 + y, 16 + group * 4 + part] = tile[:, part * 256 : (part + 1) * 256]


def tile_kernel(offsets, orbitals, own, other, out, tiles, held):
    choose_vectors(orbitals, own, other, out)
    hold_amps(own, other, held)
    chip = lax.axis_index("zl") * 4 + lax.axis_index("y")
    first = first_at(offsets, chip, lax.axis_index("core"))
    for j in range(2):
        late, slot = place_of(offsets, chip, first + 2 * j)
        for dest in range(16):
            tile = held[late, dest // 2 * 2 + slot]
            for part in range(2):
                start = dest % 2 * 512 + part * 256
                tiles[dest, j * 2 + part] = tile[:, start : start + 256]


def fill_kernel(offsets, chosen, tiles, token, local, out):
    out[:, :16] = chosen[...]
    core = lax.axis_index("core")
    for chip in range(16):
        for j in range(2):
            pair = first_at(offsets, chip, core) + 2 * j

            @pl.when(pair < offsets[chip * 2 + 2])
            def _():
                dest = ((pair & 7) >> 1) * 4 + (pair >> 3)
                for part in range(2):
                    out[dest, 16 + part] = tiles[chip, j * 2 + part]


def local_kernel(offsets, orbitals, energy, own, fock, after, out):
    owner = owner_index()
    tiles = [own[1, group * 2 + slot].astype(jnp.float32) for slot in range(2) for group in range(8)]
    both = jnp.concatenate(tiles, axis=0)
    term = jnp.dot(both.astype(jnp.bfloat16), fock[...], preferred_element_type=jnp.float32)
    for slot in range(2):
        pair = jnp.minimum(offsets[owner] + slot, 31)
        shift = energy[orbitals[0, pair]] + energy[orbitals[1, pair]]
        here = slice(slot * 64, (slot + 1) * 64)
        out[:, slot * 1024 : (slot + 1) * 1024] = term[here] - shift * both[here]


def chip_of(offsets, pair):
    chip = jnp.int32(0)
    for end in range(2, 32, 2):
        chip += (offsets[end] <= pair).astype(jnp.int32)
    return chip


def couple_kernel(offsets, case, arrived, out, rows, cols):
    zl, y, core = (lax.axis_index(name) for name in PAIR)
    swap = jnp.where(case[pair_at(zl, y, core)] == 0, 0.5, -0.5).astype(jnp.float32)
    for part in range(4):
        here = slice(part * 256, (part + 1) * 256)
        for which in range(2):
            left = arrived[:, which * 4 + part].astype(jnp.float32).reshape(128, 256)
            right = arrived[:, 8 + which * 4 + part].astype(jnp.float32).reshape(128, 256)
            start = which * 128
            rows[start : start + 128, here] = left
            rows[start + 256 : start + 384, here] = right
            cols[start : start + 128, here] = (0.5 * right).astype(jnp.bfloat16)
            cols[start + 256 : start + 384, here] = (swap * left).astype(jnp.bfloat16)
    for row in range(4):
        block = rows[:, row * 256 : (row + 1) * 256].T.astype(jnp.bfloat16)
        for part in range(4):
            there = cols[:, part * 256 : (part + 1) * 256]
            product = jnp.dot(block, there, preferred_element_type=jnp.float32)
            out[row * 4 + part, 0:256] = product.astype(jnp.bfloat16)
    for source in range(4):
        pair = pair_at(zl, source, core)
        chip = chip_of(offsets, pair)
        for part in range(4):
            tiles = [arrived[chip, 16 + group * 4 + part].astype(jnp.float32) for group in range(2)]
            tile = jnp.concatenate(tiles, axis=0).astype(jnp.bfloat16)
            for row in range(4):
                out[row * 4 + part, 256 + source * 16 : 272 + source * 16] = tile


def finish_kernel(parts, fock, out, cols):
    x, zh = lax.axis_index("x"), lax.axis_index("zh")
    cols[...] = jnp.zeros((512, 1024), jnp.bfloat16)
    for band in range(4):
        for quarter in range(4):
            start = pl.multiple_of(band * 128 + (zh & 1) * 64 + quarter * 16, 16)
            for y in range(4):
                tile = parts[band * 4 + quarter, 256 + y * 16 : 272 + y * 16]
                cols[pl.ds(start, 16), y * 256 : (y + 1) * 256] = tile
    top = pl.multiple_of(x * 256, 256)
    lanes = [pl.multiple_of((band * 2 + (zh >> 1)) * 128, 128) for band in range(4)]
    rows = jnp.concatenate([fock[pl.ds(top, 256), pl.ds(lane, 128)] for lane in lanes], axis=1)
    for y in range(4):
        total = jnp.dot(rows, cols[:, y * 256 : (y + 1) * 256], preferred_element_type=jnp.float32)
        for band in range(4):
            total += parts[band * 4 + y, 0:256].astype(jnp.float32)
        for dest in range(4):
            out[dest, y] = total[dest * 64 : (dest + 1) * 64].astype(jnp.bfloat16)


def late_couple_kernel(offsets, case, arrived, fock, out, rows, cols):
    zl = lax.axis_index("zl")
    pair = pair_at(zl, lax.axis_index("y"), lax.axis_index("core"))
    run = lax.axis_index("zh") + (zl >= 2).astype(jnp.int32)
    x, zh = lax.axis_index("x"), (run + 3 + (chip_of(offsets, pair) < 8).astype(jnp.int32)) & 3
    swap = jnp.where(case[pair] == 0, 0.5, -0.5).astype(jnp.float32)
    cols[512:640] = jnp.zeros((128, 1024), jnp.bfloat16)
    top = pl.multiple_of(512 + (zh & 1) * 64, 64)
    for part in range(4):
        here = slice(part * 256, (part + 1) * 256)
        for which in range(2):
            left = arrived[:, which * 4 + part].astype(jnp.float32).reshape(128, 256)
            right = arrived[:, 8 + which * 4 + part].astype(jnp.float32).reshape(128, 256)
            start = which * 128
            rows[start : start + 128, here] = left
            rows[start + 256 : start + 384, here] = right
            cols[start : start + 128, here] = (0.5 * right).astype(jnp.bfloat16)
            cols[start + 256 : start + 384, here] = (swap * left).astype(jnp.bfloat16)
        tiles = [arrived[group * 2 + part // 2, 16 + part % 2].astype(jnp.float32) for group in range(8)]
        cols[pl.ds(top, 64), here] = jnp.concatenate(tiles, axis=0).astype(jnp.bfloat16)
    lanes = pl.multiple_of((x * 2 + (zh >> 1)) * 128, 128)
    for row in range(4):
        here = slice(row * 256, (row + 1) * 256)
        block = jnp.concatenate([rows[:, here].T.astype(jnp.bfloat16), fock[here, pl.ds(lanes, 128)]], axis=1)
        product = jnp.dot(block, cols[...], preferred_element_type=jnp.float32)
        out[row] = product.astype(jnp.bfloat16)


def late_finish_kernel(parts, out):
    for y in range(4):
        here = slice(y * 256, (y + 1) * 256)
        total = parts[0, :, here].astype(jnp.float32)
        for x in range(1, 4):
            total += parts[x, :, here].astype(jnp.float32)
        for zh in range(4):
            out[zh * 4 + y] = total[zh * 64 : (zh + 1) * 64].astype(jnp.bfloat16)


def route_kernel(offsets, parts, out, total):
    for y in range(4):
        sums = parts[0, y].astype(jnp.float32)
        for zh in range(1, 4):
            sums += parts[zh, y].astype(jnp.float32)
        total[y] = sums.astype(jnp.bfloat16)
    member = lax.axis_index("zl") * 2 + lax.axis_index("core")
    for chip in range(16):
        end = offsets[chip * 2 + 2]
        which = jnp.maximum(((end + 7 - member) >> 3) - 1, 0)
        out[chip] = total[which]


def pick_kernel(offsets, arrived, mine, theirs):
    core, owner = lax.axis_index("core"), owner_index()
    for who, out in ((owner, mine), (owner ^ 1, theirs)):
        first = offsets[who]
        pair = first + ((first ^ core) & 1)
        for y in range(4):
            out[:, y * 256 : (y + 1) * 256] = arrived[((pair & 7) >> 1) * 4 + y]


def own_kernel(offsets, mine, local, out):
    owner = owner_index()
    first = offsets[owner]
    count = offsets[owner + 1] - first
    for slot in range(2):
        own = ((first + slot) & 1) == lax.axis_index("core")
        result = local[:, slot * 1024 : (slot + 1) * 1024] + jnp.where(own, mine[...].astype(jnp.float32), 0.0)
        out[:, slot, :] = jnp.where(slot < count, result, 0.0)


def write_kernel(offsets, base, other, out):
    owner = owner_index()
    first = offsets[owner]
    count = offsets[owner + 1] - first
    place = (first & 1) ^ lax.axis_index("core") ^ 1
    out[...] = base[...]
    for slot in range(2):

        @pl.when((place == slot) & (slot < count))
        def _():
            out[:, slot, :] = base[:, slot, :] + other[...].astype(jnp.float32)


def call(kernel, out, in_specs, *args, scratch=()):
    return pl.pallas_call(
        kernel,
        out_shape=out,
        in_specs=in_specs,
        out_specs=jax.tree.map(lambda _: VMEM, out),
        scratch_shapes=list(scratch),
        compiler_params=LIMIT,
    )(*args)


def half(*shape):
    return jax.ShapeDtypeStruct(shape, jnp.bfloat16)


def single(*shape):
    return jax.ShapeDtypeStruct(shape, jnp.float32)


def shifted(block):
    runs = [[((run + (zl < 2)) % 4 * 4 + zl) * 4 + y for zl in range(4) for y in range(4)] for run in range(4)]
    return lax.all_to_all(block, ("zh", "zl", "y"), 0, 0, axis_index_groups=runs, tiled=True)


def local_part(own, fock, orbital_energy, orbitals, owner_offsets, after):
    return call(
        local_kernel, single(64, 2048), [SMEM] * 3 + [VMEM] * 2 + [ANY],
        owner_offsets, orbitals, orbital_energy, own, fock, after,
    )


def route(parts, owner_offsets):
    return call(
        route_kernel, half(16, 64, 256), [SMEM, VMEM], owner_offsets, parts,
        scratch=[pltpu.VMEM((4, 64, 256), jnp.bfloat16)],
    )


def early_chain(own, other, fock, orbital_energy, orbitals, pair_case, owner_offsets):
    chosen = call(
        prepare_kernel, half(16, 24, 8, 256), [SMEM] * 2 + [VMEM] * 2, owner_offsets, orbitals, own, other,
        scratch=[pltpu.VMEM((2, 16, 8, 1024), jnp.bfloat16)],
    )
    arrived = lax.all_to_all(chosen, ("zl", "y"), 0, 0, tiled=True)
    partial = call(
        couple_kernel, half(16, 320, 256), [SMEM, SMEM, VMEM], owner_offsets, pair_case, arrived,
        scratch=[pltpu.VMEM((512, 1024), jnp.float32), pltpu.VMEM((512, 1024), jnp.bfloat16)],
    )
    parts = lax.all_to_all(partial, ("x", "y"), 0, 0, tiled=True)
    parts = call(
        finish_kernel, half(4, 4, 64, 256), [VMEM, VMEM], parts, fock, scratch=[pltpu.VMEM((512, 1024), jnp.bfloat16)]
    )
    parts = lax.all_to_all(parts, "zh", 0, 0, tiled=True)
    return route(parts, owner_offsets), local_part(own, fock, orbital_energy, orbitals, owner_offsets, parts)


def late_chain(own, other, fock, orbital_energy, orbitals, pair_case, owner_offsets):
    chosen, tiles = call(
        tile_kernel, [half(16, 16, 8, 256), half(16, 4, 8, 256)], [SMEM] * 2 + [VMEM] * 2,
        owner_offsets, orbitals, own, other, scratch=[pltpu.VMEM((2, 16, 8, 1024), jnp.bfloat16)],
    )
    tiles = shifted(tiles)
    token = other[0, 0, :, :128]
    for axis in TURNS:
        token = lax.ppermute(token, (axis, "core"), [(i * 2 + 1, (i + 1) % 4 * 2 + 1) for i in range(4)])
    local = local_part(own, fock, orbital_energy, orbitals, owner_offsets, tiles)
    chosen = call(
        fill_kernel, half(16, 18, 8, 256), [SMEM] + [VMEM] * 2 + [ANY] * 2, owner_offsets, chosen, tiles, token, local
    )
    arrived = shifted(chosen)
    partial = call(
        late_couple_kernel, half(4, 256, 1024), [SMEM, SMEM, VMEM, VMEM], owner_offsets, pair_case, arrived, fock,
        scratch=[pltpu.VMEM((512, 1024), jnp.float32), pltpu.VMEM((640, 1024), jnp.bfloat16)],
    )
    parts = lax.all_to_all(partial, "x", 0, 0, tiled=True)
    parts = call(late_finish_kernel, half(16, 64, 256), [VMEM], parts)
    parts = lax.all_to_all(parts, ("zh", "y"), 0, 0, tiled=True).reshape(4, 4, 64, 256)
    return route(parts, owner_offsets), local


def body(chol_vectors, amplitudes, fock, orbital_energy, pair_orbitals, pair_case, owner_offsets):
    flat = amplitudes.reshape(64, 2048)
    orbitals = pair_orbitals.T

    own = call(pack_kernel, half(2, 16, 8, 1024), [VMEM] * 2, chol_vectors, flat)
    other = lax.ppermute(own, "core", [(0, 1), (1, 0)])
    routed, local = lax.cond(
        lax.axis_index("core") == 0, early_chain, late_chain,
        own, other, fock, orbital_energy, orbitals, pair_case, owner_offsets,
    )
    arrived = lax.all_to_all(routed, ("zl", "y"), 0, 0, tiled=True)
    mine, theirs = call(pick_kernel, [half(64, 1024), half(64, 1024)], [SMEM, VMEM], owner_offsets, arrived)
    other = lax.ppermute(theirs, "core", [(0, 1), (1, 0)])
    base = call(own_kernel, single(64, 2, 1024), [SMEM] + [VMEM] * 2, owner_offsets, mine, local)
    return call(write_kernel, single(64, 2, 1024), [SMEM] + [VMEM] * 2, owner_offsets, base, other)


def solution(mesh):
    fine = Mesh(mesh.devices.reshape(4, 4, 4, 4, 2), ("x", "zh", "zl", "y", "core"))
    in_specs = (P(None, CHOL + PAIR, None), P(CHOL, PAIR, None), P(), P(), P(), P(), P())
    return jax.shard_map(body, mesh=fine, in_specs=in_specs, out_specs=P(CHOL, PAIR, None), check_vma=False)
```

```python
import jax
import jax.numpy as jnp
from jax import lax
from jax.experimental import pallas as pl
from jax.experimental.pallas import tpu as pltpu
from jax.sharding import Mesh, PartitionSpec as P

CHOL = ("x", "zh")
PAIR = ("zl", "y", "core")
VMEM = pl.BlockSpec(memory_space=pltpu.VMEM)
ANY = pl.BlockSpec(memory_space=pl.ANY)
TURNS = ("zh",)
SMEM = pl.BlockSpec(memory_space=pltpu.SMEM)
LIMIT = pltpu.CompilerParams(vmem_limit_bytes=32 * 1024 * 1024)


def pair_at(zl, y, core):
    return y * 8 + zl * 2 + core


def owner_index():
    return lax.axis_index("zl") * 8 + lax.axis_index("y") * 2 + lax.axis_index("core")


def first_at(offsets, chip, core):
    first = offsets[chip * 2]
    return first + ((first ^ core) & 1)


def pack_kernel(vectors, amps, out):
    out[0] = vectors[...]
    wide = amps[...].astype(jnp.float32)
    for group in range(8):
        for slot in range(2):
            tile = wide[group * 8 : (group + 1) * 8, slot * 1024 : (slot + 1) * 1024]
            out[1, group * 2 + slot] = tile.astype(jnp.bfloat16)


def choose_vectors(orbitals, own, other, out):
    core = lax.axis_index("core")
    for dest in range(16):
        pair = pair_at(dest // 4, dest % 4, core)
        for side in range(2):
            for which, source in enumerate((own, other)):
                chosen = source[0, orbitals[side, pair]]
                for part in range(4):
                    out[dest, side * 8 + which * 4 + part] = chosen[:, part * 256 : (part + 1) * 256]


def hold_amps(own, other, held):
    core = lax.axis_index("core")
    held[core] = own[1]
    held[1 - core] = other[1]


def place_of(offsets, chip, pair):
    start, middle = offsets[chip * 2], offsets[chip * 2 + 1]
    late = pair >= middle
    return late.astype(jnp.int32), jnp.clip(jnp.where(late, pair - middle, pair - start), 0, 1)


def prepare_kernel(offsets, orbitals, own, other, out, held):
    choose_vectors(orbitals, own, other, out)
    hold_amps(own, other, held)
    chip = lax.axis_index("zl") * 4 + lax.axis_index("y")
    first = first_at(offsets, chip, lax.axis_index("core"))
    for kind in range(4):
        pair = first + 2 * jnp.minimum((kind - (first >> 1)) & 3, 1)
        late, slot = place_of(offsets, chip, pair)
        for y in range(4):
            for group in range(2):
                tile = held[late, (y * 2 + group) * 2 + slot]
                for part in range(4):
                    out[kind * 4 + y, 16 + group * 4 + part] = tile[:, part * 256 : (part + 1) * 256]


def tile_kernel(offsets, orbitals, own, other, out, tiles, held):
    choose_vectors(orbitals, own, other, out)
    hold_amps(own, other, held)
    chip = lax.axis_index("zl") * 4 + lax.axis_index("y")
    first = first_at(offsets, chip, lax.axis_index("core"))
    for j in range(2):
        late, slot = place_of(offsets, chip, first + 2 * j)
        for dest in range(16):
            tile = held[late, dest // 2 * 2 + slot]
            for part in range(2):
                start = dest % 2 * 512 + part * 256
                tiles[dest, j * 2 + part] = tile[:, start : start + 256]


def fill_kernel(offsets, chosen, tiles, token, local, out):
    out[:, :16] = chosen[...]
    core = lax.axis_index("core")
    for chip in range(16):
        for j in range(2):
            pair = first_at(offsets, chip, core) + 2 * j

            @pl.when(pair < offsets[chip * 2 + 2])
            def _():
                dest = ((pair & 7) >> 1) * 4 + (pair >> 3)
                for part in range(2):
                    out[dest, 16 + part] = tiles[chip, j * 2 + part]


def local_kernel(offsets, orbitals, energy, own, fock, after, out):
    owner = owner_index()
    tiles = [own[1, group * 2 + slot].astype(jnp.float32) for slot in range(2) for group in range(8)]
    both = jnp.concatenate(tiles, axis=0)
    term = jnp.dot(both.astype(jnp.bfloat16), fock[...], preferred_element_type=jnp.float32)
    for slot in range(2):
        pair = jnp.minimum(offsets[owner] + slot, 31)
        shift = energy[orbitals[0, pair]] + energy[orbitals[1, pair]]
        here = slice(slot * 64, (slot + 1) * 64)
        out[:, slot * 1024 : (slot + 1) * 1024] = term[here] - shift * both[here]


def chip_of(offsets, pair):
    chip = jnp.int32(0)
    for end in range(2, 32, 2):
        chip += (offsets[end] <= pair).astype(jnp.int32)
    return chip


def couple_kernel(offsets, case, arrived, out, rows, cols):
    zl, y, core = (lax.axis_index(name) for name in PAIR)
    swap = jnp.where(case[pair_at(zl, y, core)] == 0, 0.5, -0.5).astype(jnp.float32)
    for part in range(4):
        here = slice(part * 256, (part + 1) * 256)
        for which in range(2):
            left = arrived[:, which * 4 + part].astype(jnp.float32).reshape(128, 256)
            right = arrived[:, 8 + which * 4 + part].astype(jnp.float32).reshape(128, 256)
            start = which * 128
            rows[start : start + 128, here] = left
            rows[start + 256 : start + 384, here] = right
            cols[start : start + 128, here] = (0.5 * right).astype(jnp.bfloat16)
            cols[start + 256 : start + 384, here] = (swap * left).astype(jnp.bfloat16)
    for row in range(4):
        block = rows[:, row * 256 : (row + 1) * 256].T.astype(jnp.bfloat16)
        product = jnp.dot(block, cols[...], preferred_element_type=jnp.float32).astype(jnp.bfloat16)
        for part in range(4):
            out[row * 4 + part, 0:256] = product[:, part * 256 : (part + 1) * 256]
    for source in range(4):
        pair = pair_at(zl, source, core)
        chip = chip_of(offsets, pair)
        for part in range(4):
            tiles = [arrived[chip, 16 + group * 4 + part].astype(jnp.float32) for group in range(2)]
            tile = jnp.concatenate(tiles, axis=0).astype(jnp.bfloat16)
            for row in range(4):
                out[row * 4 + part, 256 + source * 16 : 272 + source * 16] = tile


def finish_kernel(parts, fock, out, cols):
    x, zh = lax.axis_index("x"), lax.axis_index("zh")
    cols[...] = jnp.zeros((512, 1024), jnp.bfloat16)
    for band in range(4):
        for quarter in range(4):
            start = pl.multiple_of(band * 128 + (zh & 1) * 64 + quarter * 16, 16)
            for y in range(4):
                tile = parts[band * 4 + quarter, 256 + y * 16 : 272 + y * 16]
                cols[pl.ds(start, 16), y * 256 : (y + 1) * 256] = tile
    top = pl.multiple_of(x * 256, 256)
    lanes = [pl.multiple_of((band * 2 + (zh >> 1)) * 128, 128) for band in range(4)]
    rows = jnp.concatenate([fock[pl.ds(top, 256), pl.ds(lane, 128)] for lane in lanes], axis=1)
    for y in range(4):
        total = jnp.dot(rows, cols[:, y * 256 : (y + 1) * 256], preferred_element_type=jnp.float32)
        for band in range(4):
            total += parts[band * 4 + y, 0:256].astype(jnp.float32)
        for dest in range(4):
            out[dest, y] = total[dest * 64 : (dest + 1) * 64].astype(jnp.bfloat16)


def late_couple_kernel(offsets, case, arrived, fock, out, rows, cols):
    zl = lax.axis_index("zl")
    pair = pair_at(zl, lax.axis_index("y"), lax.axis_index("core"))
    run = lax.axis_index("zh") + (zl >= 2).astype(jnp.int32)
    x, zh = lax.axis_index("x"), (run + 3 + (chip_of(offsets, pair) < 8).astype(jnp.int32)) & 3
    swap = jnp.where(case[pair] == 0, 0.5, -0.5).astype(jnp.float32)
    cols[512:640] = jnp.zeros((128, 1024), jnp.bfloat16)
    top = pl.multiple_of(512 + (zh & 1) * 64, 64)
    for part in range(4):
        here = slice(part * 256, (part + 1) * 256)
        for which in range(2):
            left = arrived[:, which * 4 + part].astype(jnp.float32).reshape(128, 256)
            right = arrived[:, 8 + which * 4 + part].astype(jnp.float32).reshape(128, 256)
            start = which * 128
            rows[start : start + 128, here] = left
            rows[start + 256 : start + 384, here] = right
            cols[start : start + 128, here] = (0.5 * right).astype(jnp.bfloat16)
            cols[start + 256 : start + 384, here] = (swap * left).astype(jnp.bfloat16)
        tiles = [arrived[group * 2 + part // 2, 16 + part % 2].astype(jnp.float32) for group in range(8)]
        cols[pl.ds(top, 64), here] = jnp.concatenate(tiles, axis=0).astype(jnp.bfloat16)
    lanes = pl.multiple_of((x * 2 + (zh >> 1)) * 128, 128)
    for row in range(4):
        here = slice(row * 256, (row + 1) * 256)
        block = jnp.concatenate([rows[:, here].T.astype(jnp.bfloat16), fock[here, pl.ds(lanes, 128)]], axis=1)
        product = jnp.dot(block, cols[...], preferred_element_type=jnp.float32)
        out[row] = product.astype(jnp.bfloat16)


def late_finish_kernel(parts, out):
    for y in range(4):
        here = slice(y * 256, (y + 1) * 256)
        total = parts[0, :, here].astype(jnp.float32)
        for x in range(1, 4):
            total += parts[x, :, here].astype(jnp.float32)
        for zh in range(4):
            out[zh * 4 + y] = total[zh * 64 : (zh + 1) * 64].astype(jnp.bfloat16)


def route_kernel(offsets, parts, out, total):
    for y in range(4):
        sums = parts[0, y].astype(jnp.float32)
        for zh in range(1, 4):
            sums += parts[zh, y].astype(jnp.float32)
        total[y] = sums.astype(jnp.bfloat16)
    member = lax.axis_index("zl") * 2 + lax.axis_index("core")
    for chip in range(16):
        end = offsets[chip * 2 + 2]
        which = jnp.maximum(((end + 7 - member) >> 3) - 1, 0)
        out[chip] = total[which]


def pick_kernel(offsets, arrived, mine, theirs):
    core, owner = lax.axis_index("core"), owner_index()
    for who, out in ((owner, mine), (owner ^ 1, theirs)):
        first = offsets[who]
        pair = first + ((first ^ core) & 1)
        for y in range(4):
            out[:, y * 256 : (y + 1) * 256] = arrived[((pair & 7) >> 1) * 4 + y]


def own_kernel(offsets, mine, local, out):
    owner = owner_index()
    first = offsets[owner]
    count = offsets[owner + 1] - first
    for slot in range(2):
        own = ((first + slot) & 1) == lax.axis_index("core")
        result = local[:, slot * 1024 : (slot + 1) * 1024] + jnp.where(own, mine[...].astype(jnp.float32), 0.0)
        out[:, slot, :] = jnp.where(slot < count, result, 0.0)


def write_kernel(offsets, base, other, out):
    owner = owner_index()
    first = offsets[owner]
    count = offsets[owner + 1] - first
    place = (first & 1) ^ lax.axis_index("core") ^ 1
    out[...] = base[...]
    for slot in range(2):

        @pl.when((place == slot) & (slot < count))
        def _():
            out[:, slot, :] = base[:, slot, :] + other[...].astype(jnp.float32)


def call(kernel, out, in_specs, *args, scratch=()):
    return pl.pallas_call(
        kernel,
        out_shape=out,
        in_specs=in_specs,
        out_specs=jax.tree.map(lambda _: VMEM, out),
        scratch_shapes=list(scratch),
        compiler_params=LIMIT,
    )(*args)


def half(*shape):
    return jax.ShapeDtypeStruct(shape, jnp.bfloat16)


def single(*shape):
    return jax.ShapeDtypeStruct(shape, jnp.float32)


def shifted(block):
    runs = [[((run + (zl < 2)) % 4 * 4 + zl) * 4 + y for zl in range(4) for y in range(4)] for run in range(4)]
    return lax.all_to_all(block, ("zh", "zl", "y"), 0, 0, axis_index_groups=runs, tiled=True)


def local_part(own, fock, orbital_energy, orbitals, owner_offsets, after):
    return call(
        local_kernel, single(64, 2048), [SMEM] * 3 + [VMEM] * 2 + [ANY],
        owner_offsets, orbitals, orbital_energy, own, fock, after,
    )


def route(parts, owner_offsets):
    return call(
        route_kernel, half(16, 64, 256), [SMEM, VMEM], owner_offsets, parts,
        scratch=[pltpu.VMEM((4, 64, 256), jnp.bfloat16)],
    )


def early_chain(own, other, fock, orbital_energy, orbitals, pair_case, owner_offsets):
    chosen = call(
        prepare_kernel, half(16, 24, 8, 256), [SMEM] * 2 + [VMEM] * 2, owner_offsets, orbitals, own, other,
        scratch=[pltpu.VMEM((2, 16, 8, 1024), jnp.bfloat16)],
    )
    arrived = lax.all_to_all(chosen, ("zl", "y"), 0, 0, tiled=True)
    partial = call(
        couple_kernel, half(16, 320, 256), [SMEM, SMEM, VMEM], owner_offsets, pair_case, arrived,
        scratch=[pltpu.VMEM((512, 1024), jnp.float32), pltpu.VMEM((512, 1024), jnp.bfloat16)],
    )
    parts = lax.all_to_all(partial, ("x", "y"), 0, 0, tiled=True)
    parts = call(
        finish_kernel, half(4, 4, 64, 256), [VMEM, VMEM], parts, fock, scratch=[pltpu.VMEM((512, 1024), jnp.bfloat16)]
    )
    parts = lax.all_to_all(parts, "zh", 0, 0, tiled=True)
    return route(parts, owner_offsets), local_part(own, fock, orbital_energy, orbitals, owner_offsets, parts)


def late_chain(own, other, fock, orbital_energy, orbitals, pair_case, owner_offsets):
    chosen, tiles = call(
        tile_kernel, [half(16, 16, 8, 256), half(16, 4, 8, 256)], [SMEM] * 2 + [VMEM] * 2,
        owner_offsets, orbitals, own, other, scratch=[pltpu.VMEM((2, 16, 8, 1024), jnp.bfloat16)],
    )
    tiles = shifted(tiles)
    token = other[0, 0, :, :128]
    for axis in TURNS:
        token = lax.ppermute(token, (axis, "core"), [(i * 2 + 1, (i + 1) % 4 * 2 + 1) for i in range(4)])
    local = local_part(own, fock, orbital_energy, orbitals, owner_offsets, tiles)
    chosen = call(
        fill_kernel, half(16, 18, 8, 256), [SMEM] + [VMEM] * 2 + [ANY] * 2, owner_offsets, chosen, tiles, token, local
    )
    arrived = shifted(chosen)
    partial = call(
        late_couple_kernel, half(4, 256, 1024), [SMEM, SMEM, VMEM, VMEM], owner_offsets, pair_case, arrived, fock,
        scratch=[pltpu.VMEM((512, 1024), jnp.float32), pltpu.VMEM((640, 1024), jnp.bfloat16)],
    )
    parts = lax.all_to_all(partial, "x", 0, 0, tiled=True)
    parts = call(late_finish_kernel, half(16, 64, 256), [VMEM], parts)
    parts = lax.all_to_all(parts, ("zh", "y"), 0, 0, tiled=True).reshape(4, 4, 64, 256)
    return route(parts, owner_offsets), local


def body(chol_vectors, amplitudes, fock, orbital_energy, pair_orbitals, pair_case, owner_offsets):
    flat = amplitudes.reshape(64, 2048)
    orbitals = pair_orbitals.T

    own = call(pack_kernel, half(2, 16, 8, 1024), [VMEM] * 2, chol_vectors, flat)
    other = lax.ppermute(own, "core", [(0, 1), (1, 0)])
    routed, local = lax.cond(
        lax.axis_index("core") == 0, early_chain, late_chain,
        own, other, fock, orbital_energy, orbitals, pair_case, owner_offsets,
    )
    arrived = lax.all_to_all(routed, ("zl", "y"), 0, 0, tiled=True)
    mine, theirs = call(pick_kernel, [half(64, 1024), half(64, 1024)], [SMEM, VMEM], owner_offsets, arrived)
    other = lax.ppermute(theirs, "core", [(0, 1), (1, 0)])
    base = call(own_kernel, single(64, 2, 1024), [SMEM] + [VMEM] * 2, owner_offsets, mine, local)
    return call(write_kernel, single(64, 2, 1024), [SMEM] + [VMEM] * 2, owner_offsets, base, other)


def solution(mesh):
    fine = Mesh(mesh.devices.reshape(4, 4, 4, 4, 2), ("x", "zh", "zl", "y", "core"))
    in_specs = (P(None, CHOL + PAIR, None), P(CHOL, PAIR, None), P(), P(), P(), P(), P())
    return jax.shard_map(body, mesh=fine, in_specs=in_specs, out_specs=P(CHOL, PAIR, None), check_vma=False)
```
